768 devices in a mesh: grp: 16 (over y, core), shard: 48 (over z, x).
Axes of the slice: x: 4, y: 8, z: 12, core: 2. Of those that a mesh axis runs over, the one named last changes fastest.
Arguments:
- target: bfloat16 [6144, 128], P(('grp', 'shard')), may hold values from -6 to 6
- history: bfloat16 [6144, 128, 128], P(('grp', 'shard')), may hold values from -6 to 6
- lengths: int32 [6144], P(('grp', 'shard')), may hold values from 1 to 128, as said below
- hist_ids: int32 [6144, 128], P(('grp', 'shard')), may hold values from 0 to 98303, as said below
- block_rows: int32 [768, 48, 48], P(('grp', 'shard')), may hold values from 0 to 1023, as said below
- block_counts: int32 [768, 48], P(('grp', 'shard')), may hold values from 0 to 48, as said below
- attn_w1: bfloat16 [512, 256], replicated, may hold values from -0.25 to 0.25
- attn_b1: float32 [256], replicated, may hold values from -4 to 4
- attn_w2: bfloat16 [256, 128], replicated, may hold values from -0.375 to 0.375
- attn_b2: float32 [128], replicated, may hold values from -4 to 4
- attn_w3: float32 [128], replicated, may hold values from -3 to 3
- pooled_gradient: float32 [6144, 128], P(('grp', 'shard')), may hold values from -6 to 6
Outputs:
- table_grad: float32 [16, 98304, 128], P('grp', 'shard')
- grad_w1: float32 [512, 256], P('grp')
- grad_b1: float32 [256], P('grp')
- grad_w2: float32 [256, 128], P('grp')
- grad_b2: float32 [128], P('grp')
- grad_w3: float32 [128], P('grp')
The draws below stay inside these ranges and needn't reach their ends.
Inputs may be any that keep to these rules, and one draw needn't show every extreme that they name: Each device's 8 lengths sum to 768; one of them is 128. `hist_ids`: A history slot listed in owner o's block holds an id in o * 2048 to (o + 1) * 2048 - 1. `block_rows`: for each device and owner o, entries c < block_counts[o] are distinct live slots b * 128 + j (j < lengths[b]) of that device's own samples; every live slot stands in exactly one owner's block; other entries are 0. `block_counts`: A device's counts sum to 768; in each grp index one owner receives 48 slots from every device; every other count of a device is at most 24, and each device has one count of exactly 24.
All inputs are finite; a program needn't handle non-finite values.
Results may differ from the reference program's by a relative error of at most 0.0067.
Values sent between devices are 32-bit elements; how exact they have to be, the bound alone decides.
No kernel may reach another device: no remote copies, remote signals or barrier semaphores. Data moves between devices by JAX's collectives and lax.ppermute only.
A program may use at most 32 MiB of HBM per device.

```python
import jax
import jax.numpy as jnp
from jax import lax

E = 128
H1 = 256
H2 = 128
FEAT = 512
B_DEV = 8
L = 128
ROWS_DEV = 2048
SENDERS = 768
OWNERS = 48
GROUPS = 16
BATCH = 6144
ITEMS = 98304
VALID_DEV = 768
CAP = 48
HALF = 24


def joint_draw(key):

    def one(dev):
        kdev = jax.random.fold_in(key, dev)
        grpidx = dev // OWNERS
        kgrp = jax.random.fold_in(jax.random.fold_in(key, 100003), grpidx)
        hot_owner = jax.random.randint(kgrp, (), 0, OWNERS)
        rest = VALID_DEV - L
        base = rest // (B_DEV - 1)
        extra = rest % (B_DEV - 1)
        others = base + (jnp.arange(B_DEV - 1) < extra).astype(jnp.int32)
        npair = (B_DEV - 1) // 2
        if npair > 0:
            moved = jax.random.randint(jax.random.fold_in(kdev, 1), (npair,), 0, min(base // 2, L - base - 1) + 1)
            delta = jnp.zeros((B_DEV - 1,), jnp.int32).at[0:2 * npair:2].add(moved).at[1:2 * npair:2].add(-moved)
            others = others + delta
        lens_rank = jnp.concatenate([jnp.full((1,), L, jnp.int32), others.astype(jnp.int32)])
        sperm = jax.random.permutation(jax.random.fold_in(kdev, 2), B_DEV)
        lens_out = jnp.zeros((B_DEV,), jnp.int32).at[sperm].set(lens_rank)
        rest2 = VALID_DEV - CAP - HALF
        base2 = rest2 // (OWNERS - 2)
        extra2 = rest2 % (OWNERS - 2)
        others2 = base2 + (jnp.arange(OWNERS - 2) < extra2).astype(jnp.int32)
        npair2 = (OWNERS - 2) // 2
        if npair2 > 0:
            moved2 = jax.random.randint(jax.random.fold_in(kdev, 3), (npair2,), 0, max(min(base2 // 2, HALF - base2 - 2), 0) + 1)
            delta2 = jnp.zeros((OWNERS - 2,), jnp.int32).at[0:2 * npair2:2].add(moved2).at[1:2 * npair2:2].add(-moved2)
            others2 = others2 + delta2
        counts_rank = jnp.concatenate([jnp.full((1,), CAP, jnp.int32), jnp.full((1,), HALF, jnp.int32), others2.astype(jnp.int32)])
        operm = jax.random.permutation(jax.random.fold_in(kdev, 4), OWNERS).astype(jnp.int32)
        where_hot = jnp.argmax((operm == hot_owner).astype(jnp.int32))
        operm = operm.at[where_hot].set(operm[0]).at[0].set(hot_owner)
        counts = jnp.zeros((OWNERS,), jnp.int32).at[operm].set(counts_rank)
        total = B_DEV * L
        posit = jnp.arange(total, dtype=jnp.int32)
        valid = posit % L < lens_out[posit // L]
        shuffle = jax.random.permutation(jax.random.fold_in(kdev, 5), total).astype(jnp.int32)
        order = jnp.argsort(jnp.where(valid, 0, total) + shuffle, stable=True).astype(jnp.int32)
        ends = jnp.cumsum(counts)
        starts = ends - counts
        slots = starts[:, None] + jnp.arange(CAP, dtype=jnp.int32)[None, :]
        used = jnp.arange(CAP, dtype=jnp.int32)[None, :] < counts[:, None]
        blocks = jnp.where(used, order[jnp.clip(slots, 0, total - 1)], 0)
        rank = jnp.arange(total, dtype=jnp.int32)
        owner_rank = jnp.sum((rank[:, None] >= ends[None, :]).astype(jnp.int32), axis=1)
        stray = jax.random.randint(jax.random.fold_in(kdev, 6), (total,), 0, OWNERS)
        owner_rank = jnp.where(rank < VALID_DEV, owner_rank, stray)
        owner_pos = jnp.zeros((total,), jnp.int32).at[order].set(owner_rank)
        hotset = jax.random.randint(jax.random.fold_in(key, 7), (8,), 0, ROWS_DEV)
        coin = jax.random.randint(jax.random.fold_in(kdev, 8), (total,), 0, 4)
        pick = jax.random.randint(jax.random.fold_in(kdev, 9), (total,), 0, 8)
        drawn = jax.random.randint(jax.random.fold_in(kdev, 10), (total,), 0, ROWS_DEV)
        hot_rows = jnp.sum(jnp.where(pick[:, None] == jnp.arange(8)[None, :], hotset[None, :], 0), axis=1)
        row_pick = jnp.where(coin == 0, hot_rows, drawn)
        ids = owner_pos * ROWS_DEV + row_pick
        return (lens_out, ids.reshape(B_DEV, L), blocks, counts)
    return jax.vmap(one)(jnp.arange(SENDERS, dtype=jnp.int32))


def draw_lengths(key, part):
    shared = joint_draw(key)
    return shared[0].reshape(BATCH).astype(jnp.int32)


def draw_hist_ids(key, part):
    shared = joint_draw(key)
    return shared[1].reshape(BATCH, L).astype(jnp.int32)


def draw_block_rows(key, part):
    shared = joint_draw(key)
    return shared[2].astype(jnp.int32)


def draw_block_counts(key, part):
    shared = joint_draw(key)
    return shared[3].astype(jnp.int32)


def block_scale(stream_key, shape, cuts, least, largest):
    def one(position, blocks):
        steps = jax.random.uniform(jax.random.fold_in(jax.random.fold_in(stream_key, 6), position), (blocks,), jnp.float32, least / len(cuts), largest / len(cuts))
        return jnp.repeat(jnp.exp(steps), shape[position] // blocks).reshape((-1,) + (1,) * (len(shape) - position - 1))

    gain = one(*cuts[0])
    for cut in cuts[1:]:
        gain = gain * one(*cut)
    return gain


def centred(stream_key, shape, scale, most, pieces=(), held_as=jnp.bfloat16):
    loudness = block_scale(stream_key, shape, pieces, -0.22, 0.18) if pieces else 1.0
    values = jax.random.normal(stream_key, shape, jnp.float32) * scale * loudness
    return jnp.minimum(jnp.maximum(values, -most), most).astype(held_as)


def setup_inputs(seed: int = 0) -> dict:
    arg_keys = jax.random.split(jax.random.key(seed), 13)
    return {
        "target": centred(arg_keys[0], (BATCH, E), 1.0, 6.0, ((0, 768),)),
        "history": centred(arg_keys[1], (BATCH, L, E), 1.0, 6.0, ((0, 768),)),
        "lengths": draw_lengths(jax.random.fold_in(arg_keys[12], 71), 0),
        "hist_ids": draw_hist_ids(jax.random.fold_in(arg_keys[12], 71), 0),
        "block_rows": draw_block_rows(jax.random.fold_in(arg_keys[12], 71), 0),
        "block_counts": draw_block_counts(jax.random.fold_in(arg_keys[12], 71), 0),
        "attn_w1": centred(arg_keys[6], (FEAT, H1), FEAT ** -0.5, 0.25),
        "attn_b1": centred(arg_keys[7], (H1,), 0.7, 4.0, (), jnp.float32),
        "attn_w2": centred(arg_keys[8], (H1, H2), H1 ** -0.5, 0.375),
        "attn_b2": centred(arg_keys[9], (H2,), 0.7, 4.0, (), jnp.float32),
        "attn_w3": centred(arg_keys[10], (H2,), 0.5, 3.0, (), jnp.float32),
        "pooled_gradient": centred(arg_keys[11], (BATCH, E), 1.0, 6.0, ((0, 768),), jnp.float32),
    }


def local_terms(target, history, lengths, pooled_gradient, attn_w1, attn_b1, attn_w2, attn_b2, attn_w3):
    sample_count, slot_count, feature_width = history.shape
    query = target.astype(jnp.float32)[:, None, :]
    hist = history.astype(jnp.float32)
    item_minus_target = (query - hist).astype(jnp.bfloat16)
    item_times_target = (query * hist).astype(jnp.bfloat16)
    query_tile = jnp.broadcast_to(target[:, None, :], history.shape)
    feature_rows = jnp.concatenate([query_tile, history, item_minus_target, item_times_target], axis=-1).reshape(sample_count * slot_count, 4 * feature_width)
    act1 = jax.nn.sigmoid(jnp.dot(feature_rows, attn_w1, preferred_element_type=jnp.float32) + attn_b1)
    act1_low = act1.astype(jnp.bfloat16)
    act2 = jax.nn.sigmoid(jnp.dot(act1_low, attn_w2, preferred_element_type=jnp.float32) + attn_b2)
    live_mask = (jnp.arange(slot_count, dtype=jnp.int32)[None, :] < lengths[:, None]).reshape(-1)
    attention_score = jnp.where(live_mask, jnp.sum(act2 * attn_w3, axis=-1), 0.0)
    dscore = jnp.sum(pooled_gradient[:, None, :] * hist, axis=-1).reshape(-1)
    dscore = jnp.where(live_mask, dscore, 0.0)
    dz2_full = dscore[:, None] * attn_w3[None, :] * act2 * (1.0 - act2)
    dz2 = dz2_full.astype(jnp.bfloat16)
    grad_w3 = jnp.sum(dscore[:, None] * act2, axis=0)
    grad_b2 = jnp.sum(dz2_full, axis=0)
    grad_w2 = jnp.dot(act1_low.T, dz2, preferred_element_type=jnp.float32)
    dz1_full = jnp.dot(dz2, attn_w2.T, preferred_element_type=jnp.float32) * act1 * (1.0 - act1)
    dz1 = dz1_full.astype(jnp.bfloat16)
    grad_b1 = jnp.sum(dz1_full, axis=0)
    grad_w1 = jnp.dot(feature_rows.T, dz1, preferred_element_type=jnp.float32)
    dfeat = jnp.dot(dz1, attn_w1.T, preferred_element_type=jnp.float32)
    part_h = dfeat[:, feature_width:2 * feature_width]
    part_d = dfeat[:, 2 * feature_width:3 * feature_width]
    part_p = dfeat[:, 3 * feature_width:]
    qflat = jnp.broadcast_to(query, hist.shape).reshape(-1, feature_width)
    pooled_contribution = (attention_score.reshape(sample_count, slot_count)[:, :, None] * pooled_gradient[:, None, :]).reshape(-1, feature_width)
    drow = part_h - part_d + part_p * qflat + pooled_contribution
    return drow, (grad_w1, grad_b1, grad_w2, grad_b2, grad_w3)


def reference(target, history, lengths, hist_ids, block_rows, block_counts, attn_w1, attn_b1, attn_w2, attn_b2, attn_w3, pooled_gradient):
    tg = target.reshape(GROUPS, OWNERS, B_DEV, E)
    hs = history.reshape(GROUPS, OWNERS, B_DEV, L, E)
    ln = lengths.reshape(GROUPS, OWNERS, B_DEV)
    ids = hist_ids.reshape(GROUPS, OWNERS, B_DEV * L)
    blk = block_rows.reshape(GROUPS, OWNERS, OWNERS, CAP)
    cnt = block_counts.reshape(GROUPS, OWNERS, OWNERS)
    gp = pooled_gradient.reshape(GROUPS, OWNERS, B_DEV, E)

    def group_fn(group_args):
        def device_step(carry, dev_args):
            table, sums = carry
            t_d, h_d, l_d, i_d, b_d, c_d, g_d = dev_args
            drow, grads = local_terms(t_d, h_d, l_d, g_d, attn_w1, attn_b1, attn_w2, attn_b2, attn_w3)
            live_mask = jnp.arange(CAP, dtype=jnp.int32)[None, :] < c_d[:, None]
            rows = jnp.where(live_mask[:, :, None], drow[b_d], 0.0)
            target_row = jnp.arange(OWNERS, dtype=jnp.int32)[:, None] * ROWS_DEV + i_d[b_d] % ROWS_DEV
            table = table.at[target_row.reshape(-1)].add(rows.reshape(-1, E))
            sums = tuple(a + b for a, b in zip(sums, grads))
            return (table, sums), None

        zeros_sums = (jnp.zeros((FEAT, H1), jnp.float32), jnp.zeros((H1,), jnp.float32),
                      jnp.zeros((H1, H2), jnp.float32), jnp.zeros((H2,), jnp.float32),
                      jnp.zeros((H2,), jnp.float32))
        init = (jnp.zeros((ITEMS, E), jnp.float32), zeros_sums)
        (table, sums), _ = lax.scan(device_step, init, group_args)
        return table, sums

    tables, sums = lax.map(group_fn, (tg, hs, ln, ids, blk, cnt, gp))
    totals = tuple(jnp.sum(s, axis=0) for s in sums)
    return tables, totals[0], totals[1], totals[2], totals[3], totals[4]
```

```python
import jax
import jax.numpy as jnp
from jax import lax
from jax.experimental import pallas as pl
from jax.experimental.pallas import tpu as pltpu
from jax.sharding import PartitionSpec as P

ROWS_DEV = 2048
E = 128
OWNERS = 48
HALF = 24
BLOCK = 32
NX = 4
PIECE = 6
SLOTS = 1024
VMEM_LIMIT = 48 * 1024 * 1024


def local_terms(
    target, history, lengths, pooled_gradient, attn_w1, attn_b1, attn_w2, attn_b2, attn_w3
):
    sample_count, slot_count, feature_width = history.shape
    query = target.astype(jnp.float32)[:, None, :]
    hist = history.astype(jnp.float32)
    item_minus_target = (query - hist).astype(jnp.bfloat16)
    item_times_target = (query * hist).astype(jnp.bfloat16)
    query_tile = jnp.broadcast_to(target[:, None, :], history.shape)
    feature_rows = jnp.concatenate(
        [query_tile, history, item_minus_target, item_times_target], axis=-1
    ).reshape(sample_count * slot_count, 4 * feature_width)
    act1 = jax.nn.sigmoid(
        jnp.dot(feature_rows, attn_w1, preferred_element_type=jnp.float32) + attn_b1
    )
    act1_low = act1.astype(jnp.bfloat16)
    act2 = jax.nn.sigmoid(jnp.dot(act1_low, attn_w2, preferred_element_type=jnp.float32) + attn_b2)
    live_mask = (jnp.arange(slot_count, dtype=jnp.int32)[None, :] < lengths[:, None]).reshape(-1)
    attention_score = jnp.where(live_mask, jnp.sum(act2 * attn_w3, axis=-1), 0.0)
    dscore = jnp.sum(pooled_gradient[:, None, :] * hist, axis=-1).reshape(-1)
    dscore = jnp.where(live_mask, dscore, 0.0)
    dz2_full = dscore[:, None] * attn_w3[None, :] * act2 * (1.0 - act2)
    dz2 = dz2_full.astype(jnp.bfloat16)
    grad_w3 = jnp.sum(dscore[:, None] * act2, axis=0)
    grad_b2 = jnp.sum(dz2_full, axis=0)
    grad_w2 = jnp.dot(act1_low.T, dz2, preferred_element_type=jnp.float32)
    dz1_full = jnp.dot(dz2, attn_w2.T, preferred_element_type=jnp.float32) * act1 * (1.0 - act1)
    dz1 = dz1_full.astype(jnp.bfloat16)
    grad_b1 = jnp.sum(dz1_full, axis=0)
    grad_w1 = jnp.dot(feature_rows.T, dz1, preferred_element_type=jnp.float32)
    dfeat = jnp.dot(dz1, attn_w1.T, preferred_element_type=jnp.float32)
    part_h = dfeat[:, feature_width : 2 * feature_width]
    part_d = dfeat[:, 2 * feature_width : 3 * feature_width]
    part_p = dfeat[:, 3 * feature_width :]
    qflat = jnp.broadcast_to(query, hist.shape).reshape(-1, feature_width)
    pooled_contribution = (
        attention_score.reshape(sample_count, slot_count)[:, :, None] * pooled_gradient[:, None, :]
    ).reshape(-1, feature_width)
    drow = part_h - part_d + part_p * qflat + pooled_contribution
    return (drow, (grad_w1, grad_b1, grad_w2, grad_b2, grad_w3))


def iota(shape, dim):
    return lax.broadcasted_iota(jnp.int32, shape, dim)


def split(rows):
    high = rows.astype(jnp.bfloat16)
    low = (rows - high.astype(jnp.float32)).astype(jnp.bfloat16)
    return jnp.concatenate([high, low], axis=1)


def pack_kernel(me_ref, counts_ref, drow_ref, ids_ref, blocks_ref, send_ref, pick, source):
    me = me_ref[0]
    hot = jnp.int32(0)
    for o in range(OWNERS):
        hot = jnp.where(counts_ref[0, o] > HALF, jnp.int32(o), hot)

    source[:, : 2 * E] = split(drow_ref[...])
    ids = ids_ref[...] & (ROWS_DEV - 1)
    id_columns = jnp.transpose(ids.astype(jnp.float32))
    for b in range(8):
        column = jnp.broadcast_to(id_columns[:, b : b + 1], (128, 128)).astype(jnp.int32)
        source[b * 128 : (b + 1) * 128, 2 * E : 3 * E] = (column >> 8).astype(jnp.float32).astype(jnp.bfloat16)
        source[b * 128 : (b + 1) * 128, 3 * E :] = (column & 255).astype(jnp.float32).astype(jnp.bfloat16)

    slot = iota((8, SLOTS), 1).astype(jnp.float32)[:1]
    eye = iota((HALF, OWNERS), 0) == iota((HALF, OWNERS), 1)
    def one_hot(mask, row):
        chosen = jnp.where(mask, row.astype(jnp.float32), 0.0)
        column = jnp.sum(chosen, axis=1, keepdims=True)
        return jnp.where(column == slot, 1.0, 0.0)
    for o in range(0, OWNERS, 2):
        pair = [one_hot(eye, blocks_ref[k : k + 1, :]) for k in (o, o + 1)]
        pick[o * HALF : (o + 2) * HALF, :] = jnp.concatenate(pair, axis=0).astype(jnp.bfloat16)
    r, lane = iota((32, OWNERS), 0), iota((32, OWNERS), 1)
    late = (lane == HALF + PIECE * (r // 8) + r % 8) & (r % 8 < PIECE)
    last = one_hot(late, blocks_ref[pl.ds(hot, 1), :])
    pick[OWNERS * HALF :, :] = last.astype(jnp.bfloat16)

    got = jnp.dot(pick[...], source[...], preferred_element_type=jnp.float32)

    sub, lane = iota((HALF, E), 0), iota((HALF, E), 1)
    place = lane - sub == (me % NX) * BLOCK
    sub8, lane8 = iota((8, E), 0), iota((8, E), 1)
    place8 = (lane8 - sub8 == (me % 16) * 8) & (sub8 < PIECE)
    tails = []
    for x in range(NX):
        part = got[OWNERS * HALF + 8 * x : OWNERS * HALF + 8 * x + 8]
        where_to = part[:, 2 * E : 3 * E] * 256.0 + part[:, 3 * E :] + 1.0
        row = jnp.sum(jnp.where(place8, where_to, 0.0), axis=0, keepdims=True)
        tails.append(jnp.where(sub8 < PIECE, part[:, :E] + part[:, E : 2 * E], row))
    for o in range(OWNERS):
        part = got[o * HALF : (o + 1) * HALF]
        send_ref[o, :HALF, :] = part[:, :E] + part[:, E : 2 * E]
        where_to = part[:, 2 * E : 3 * E] * 256.0 + part[:, 3 * E :] + 1.0
        used = place & (sub < counts_ref[0, o])
        row = jnp.sum(jnp.where(used, where_to, 0.0), axis=0, keepdims=True)
        send_ref[o, HALF:, :] = jnp.where(sub8 == PIECE, row, tails[o % NX])


def pack(me, counts, drow, ids, blocks):
    whole = pl.BlockSpec(memory_space=pltpu.VMEM)
    scalar = pl.BlockSpec(memory_space=pltpu.SMEM)
    return pl.pallas_call(
        pack_kernel,
        out_shape=jax.ShapeDtypeStruct((OWNERS, BLOCK, E), jnp.float32),
        in_specs=[scalar, scalar, whole, whole, whole],
        out_specs=whole,
        scratch_shapes=[
            pltpu.VMEM((OWNERS * HALF + 32, SLOTS), jnp.bfloat16),
            pltpu.VMEM((SLOTS, 4 * E), jnp.bfloat16),
        ],
        compiler_params=pltpu.CompilerParams(vmem_limit_bytes=VMEM_LIMIT),
        cost_estimate=pl.CostEstimate(
            flops=2 * 1184 * 1024 * 512, bytes_accessed=2_000_000, transcendentals=0
        ),
        name="pack",
    )(me, counts, drow, ids, blocks)


STEP = 512


def add_kernel(me_ref, counts_ref, got_ref, late0_ref, late1_ref, late2_ref, table_ref, rows, dest):
    groups = OWNERS // NX
    for g in range(groups):
        rows[g * 128 : (g + 1) * 128, :] = split(got_ref[g * 128 : (g + 1) * 128, :])
        total = sum(got_ref[(NX * g + j) * BLOCK + HALF : (NX * g + j + 1) * BLOCK, :] for j in range(NX))
        dest[:, g * 128 : (g + 1) * 128] = jnp.broadcast_to(total[PIECE : PIECE + 1, :], (8, E))

    def product(t):
        table_row = (iota((STEP, E), 0) + (t * STEP + 1)).astype(jnp.float32)
        hits = [
            jnp.where(table_row == dest[0:1, g * 128 : (g + 1) * 128], 1.0, 0.0).astype(jnp.bfloat16)
            for g in range(groups)
        ]
        both = jnp.dot(jnp.concatenate(hits, axis=1), rows[...], preferred_element_type=jnp.float32)
        return both[:, :E] + both[:, E:]

    for t in range(ROWS_DEV // STEP):
        table_ref[t * STEP : (t + 1) * STEP, :] = product(t)

    @pl.when(counts_ref[0, me_ref[0]] > HALF)
    def _():
        for k in range(NX):
            for g in range(3):
                if k == 0:
                    tiles = [
                        got_ref[s * BLOCK + HALF : (s + 1) * BLOCK, :]
                        for s in range(16 * g, 16 * g + 16)
                    ]
                else:
                    late = (late0_ref, late1_ref, late2_ref)[k - 1]
                    tiles = [late[s * 8 : s * 8 + 8, :] for s in range(16 * g, 16 * g + 16)]
                at = (k * 3 + g) * 128
                rows[at : at + 128, :] = split(jnp.concatenate(tiles, axis=0))
                dest[:, at : at + 128] = jnp.broadcast_to(sum(tiles)[7:8, :], (8, E))
        for t in range(ROWS_DEV // STEP):
            table_ref[t * STEP : (t + 1) * STEP, :] += product(t)


def add_rows(me, counts, got, late):
    whole = pl.BlockSpec(memory_space=pltpu.VMEM)
    scalar = pl.BlockSpec(memory_space=pltpu.SMEM)
    return pl.pallas_call(
        add_kernel,
        out_shape=jax.ShapeDtypeStruct((ROWS_DEV, E), jnp.float32),
        in_specs=[scalar, scalar, whole, whole, whole, whole],
        out_specs=whole,
        scratch_shapes=[
            pltpu.VMEM((OWNERS * BLOCK, 2 * E), jnp.bfloat16),
            pltpu.VMEM((8, OWNERS * BLOCK), jnp.float32),
        ],
        compiler_params=pltpu.CompilerParams(vmem_limit_bytes=VMEM_LIMIT),
        cost_estimate=pl.CostEstimate(
            flops=2 * 2048 * 1536 * 256, bytes_accessed=2_500_000, transcendentals=0
        ),
        name="add_rows",
    )(me, counts, got, *late)


def grp_swap(bit):
    return [(g, g ^ bit) for g in range(16)]


def shard_swap(bit):
    return [(s, s ^ bit) for s in range(OWNERS)]


def shard_turn(step):
    return [(s, (s + step) % OWNERS) for s in range(OWNERS)]


def x_turn(step):
    return [(s, s // NX * NX + (s + step) % NX) for s in range(OWNERS)]


def sum_grads(grads, g):
    w1, b1, w2, b2, w3 = grads
    small = jnp.concatenate([b1.reshape(16, 16), b2.reshape(16, 8), w3.reshape(16, 8)], axis=1)
    small = jnp.pad(small[:, None, :], ((0, 0), (0, 7), (0, 96)))
    part = jnp.concatenate(
        [
            w1[:, :E].reshape(16, 32, E),
            w1[:, E:].reshape(16, 32, E),
            w2.reshape(16, 16, E),
            small,
        ],
        axis=1,
    )
    part = part.reshape(2, 2, 2, 2, 88, E).transpose(3, 2, 1, 0, 4, 5)
    for k in range(4):
        bit = (g >> k) & 1
        keep = lax.dynamic_index_in_dim(part, bit, 0, False)
        send = lax.dynamic_index_in_dim(part, 1 - bit, 0, False)
        part = keep + lax.ppermute(send, "grp", grp_swap(1 << k))
    for bit in (1, 2, 4, 8):
        part = part + lax.ppermute(part, "shard", shard_swap(bit))
    return part + lax.ppermute(part, "shard", shard_turn(16)) + lax.ppermute(part, "shard", shard_turn(32))


def shards(
    target,
    history,
    lengths,
    hist_ids,
    block_rows,
    block_counts,
    attn_w1,
    attn_b1,
    attn_w2,
    attn_b2,
    attn_w3,
    pooled_gradient,
):
    g = lax.axis_index("grp")
    me = lax.axis_index("shard").reshape(1)
    drow, grads = local_terms(
        target, history, lengths, pooled_gradient, attn_w1, attn_b1, attn_w2, attn_b2, attn_w3
    )
    send = pack(me, block_counts, drow, hist_ids, block_rows[0])
    got = lax.all_to_all(send, "shard", split_axis=0, concat_axis=0, tiled=True)
    slab = got[:, HALF:, :].reshape(OWNERS * 8, E)
    late = [lax.ppermute(slab, "shard", x_turn(step)) for step in (1, 2, 3)]
    table = add_rows(me, block_counts, got.reshape(OWNERS * BLOCK, E), late)
    share = sum_grads(grads, g)
    return (
        table[None],
        jnp.concatenate([share[:32], share[32:64]], axis=1),
        share[80, :16],
        share[64:80],
        share[80, 16:24],
        share[80, 24:32],
    )


def solution(mesh):
    placed = (
        P(("grp", "shard"), None),
        P(("grp", "shard"), None, None),
        P(("grp", "shard")),
        P(("grp", "shard"), None),
        P(("grp", "shard"), None, None),
        P(("grp", "shard"), None),
        P(),
        P(),
        P(),
        P(),
        P(),
        P(("grp", "shard"), None),
    )
    return jax.shard_map(
        shards,
        mesh=mesh,
        in_specs=placed,
        out_specs=(
            P("grp", "shard", None),
            P("grp", None),
            P("grp"),
            P("grp", None),
            P("grp"),
            P("grp"),
        ),
        check_vma=False,
    )
```

```python
import jax
import jax.numpy as jnp
from jax import lax
from jax.experimental import pallas as pl
from jax.experimental.pallas import tpu as pltpu
from jax.sharding import PartitionSpec as P

ROWS_DEV = 2048
E = 128
OWNERS = 48
HALF = 24
BLOCK = 32
NX = 4
PIECE = 6
SLOTS = 1024
VMEM_LIMIT = 24 * 1024 * 1024


def iota(shape, dim):
    return lax.broadcasted_iota(jnp.int32, shape, dim)


def split(rows):
    high = rows.astype(jnp.bfloat16)
    low = (rows - high.astype(jnp.float32)).astype(jnp.bfloat16)
    return jnp.concatenate([high, low], axis=1)


CHUNK = 256
PART = 88


def sigmoid(z):
    return 0.5 * jnp.tanh(0.5 * z) + 0.5


def places():
    at = []
    for g in range(16):
        core, y0, y1, y2 = g & 1, (g >> 1) & 1, (g >> 2) & 1, (g >> 3) & 1
        at.append(core * 8 + (y0 ^ y2) * 4 + (y1 ^ y2) * 2 + y2)
    return at


def dense_kernel(
    lengths_ref, target_ref, hist_ref, pg_ref, w1_ref, b1_ref, w2_ref, b2_ref, w3_ref,
    drow_ref, part_ref, feats, act1s, dz2s, dz1s,
):
    query = target_ref[...].astype(jnp.float32)
    w1, w2, w3 = w1_ref[...], w2_ref[...], w3_ref[...]
    grad_w3 = jnp.zeros((1, E), jnp.float32)
    grad_b2 = jnp.zeros((1, E), jnp.float32)
    grad_b1 = jnp.zeros((1, 2 * E), jnp.float32)
    samples = CHUNK // 128
    across = (((1,), (1,)), ((), ()))
    down = (((0,), (0,)), ((), ()))
    for c in range(SLOTS // CHUNK):
        rows = slice(c * CHUNK, (c + 1) * CHUNK)
        hist_low = hist_ref[rows, :]
        hist = hist_low.astype(jnp.float32)
        def spread(rows_of):
            parts = [rows_of[b : b + 1, :] for b in range(c * samples, (c + 1) * samples)]
            return jnp.concatenate([jnp.broadcast_to(v, (128, E)) for v in parts], axis=0)
        q = spread(query)
        pg = spread(pg_ref)
        live = jnp.concatenate(
            [iota((128, 1), 0) < lengths_ref[b] for b in range(c * samples, (c + 1) * samples)], axis=0
        )
        feat = jnp.concatenate(
            [q.astype(jnp.bfloat16), hist_low, (q - hist).astype(jnp.bfloat16), (q * hist).astype(jnp.bfloat16)],
            axis=1,
        )
        feats[rows, :] = feat
        act1 = sigmoid(jnp.dot(feat, w1, preferred_element_type=jnp.float32) + b1_ref[...])
        act1_low = act1.astype(jnp.bfloat16)
        act1s[rows, :] = act1_low
        act2 = sigmoid(jnp.dot(act1_low, w2, preferred_element_type=jnp.float32) + b2_ref[...])
        score = jnp.where(live, jnp.sum(act2 * w3, axis=1, keepdims=True), 0.0)
        dscore = jnp.where(live, jnp.sum(pg * hist, axis=1, keepdims=True), 0.0)
        dact2 = dscore * act2
        grad_w3 += jnp.sum(dact2, axis=0, keepdims=True)
        dz2_full = dact2 * w3 * (1.0 - act2)
        grad_b2 += jnp.sum(dz2_full, axis=0, keepdims=True)
        dz2 = dz2_full.astype(jnp.bfloat16)
        dz2s[rows, :] = dz2
        back = lax.dot_general(dz2, w2, across, preferred_element_type=jnp.float32)
        dz1_full = back * act1 * (1.0 - act1)
        grad_b1 += jnp.sum(dz1_full, axis=0, keepdims=True)
        dz1 = dz1_full.astype(jnp.bfloat16)
        dz1s[rows, :] = dz1
        dfeat = lax.dot_general(dz1, w1[E:, :], across, preferred_element_type=jnp.float32)
        drow_ref[rows, :] = dfeat[:, :E] - dfeat[:, E : 2 * E] + dfeat[:, 2 * E :] * q + score * pg

    grad_w1 = lax.dot_general(feats[...], dz1s[...], down, preferred_element_type=jnp.float32)
    grad_w2 = lax.dot_general(act1s[...], dz2s[...], down, preferred_element_type=jnp.float32)
    sub = iota((8, E), 0)
    small = jnp.where(sub == 0, grad_b1[:, :E], jnp.where(sub == 1, grad_b1[:, E:], 0.0))
    small = jnp.where(sub == 2, grad_b2, jnp.where(sub == 3, grad_w3, small))
    for g, at in enumerate(places()):
        base = at * PART
        part_ref[base : base + 32, :] = grad_w1[32 * g : 32 * g + 32, :E]
        part_ref[base + 32 : base + 64, :] = grad_w1[32 * g : 32 * g + 32, E:]
        part_ref[base + 64 : base + 80, :] = grad_w2[16 * g : 16 * g + 16, :]
        part_ref[base + 80 : base + 88, :] = small


def dense(lengths, target, hist, pg, w1, b1, w2, b2, w3):
    whole = pl.BlockSpec(memory_space=pltpu.VMEM)
    scalar = pl.BlockSpec(memory_space=pltpu.SMEM)
    return pl.pallas_call(
        dense_kernel,
        out_shape=[
            jax.ShapeDtypeStruct((SLOTS, E), jnp.float32),
            jax.ShapeDtypeStruct((16 * PART, E), jnp.float32),
        ],
        in_specs=[scalar] + [whole] * 8,
        out_specs=[whole, whole],
        scratch_shapes=[
            pltpu.VMEM((SLOTS, 4 * E), jnp.bfloat16),
            pltpu.VMEM((SLOTS, 2 * E), jnp.bfloat16),
            pltpu.VMEM((SLOTS, E), jnp.bfloat16),
            pltpu.VMEM((SLOTS, 2 * E), jnp.bfloat16),
        ],
        compiler_params=pltpu.CompilerParams(vmem_limit_bytes=VMEM_LIMIT),
        cost_estimate=pl.CostEstimate(
            flops=1_100_000_000, bytes_accessed=2_200_000, transcendentals=400_000
        ),
        name="dense",
    )(lengths, target, hist, pg, w1, b1, w2, b2, w3)


def pack_kernel(me_ref, counts_ref, drow_ref, ids_ref, blocks_ref, send_ref, pick, source):
    me = me_ref[0]
    hot = jnp.int32(0)
    for o in range(OWNERS):
        hot = jnp.where(counts_ref[0, o] > HALF, jnp.int32(o), hot)

    source[:, : 2 * E] = split(drow_ref[...])
    ids = ids_ref[...] & (ROWS_DEV - 1)
    id_columns = jnp.transpose(ids.astype(jnp.float32))
    for b in range(8):
        column = jnp.broadcast_to(id_columns[:, b : b + 1], (128, 128)).astype(jnp.int32)
        source[b * 128 : (b + 1) * 128, 2 * E : 3 * E] = (column >> 8).astype(jnp.float32).astype(jnp.bfloat16)
        source[b * 128 : (b + 1) * 128, 3 * E :] = (column & 255).astype(jnp.float32).astype(jnp.bfloat16)

    slot = iota((8, SLOTS), 1).astype(jnp.float32)[:1]
    eye = iota((HALF, OWNERS), 0) == iota((HALF, OWNERS), 1)
    def one_hot(mask, row):
        chosen = jnp.where(mask, row.astype(jnp.float32), 0.0)
        column = jnp.sum(chosen, axis=1, keepdims=True)
        return jnp.where(column == slot, 1.0, 0.0)
    for o in range(0, OWNERS, 2):
        pair = [one_hot(eye, blocks_ref[k : k + 1, :]) for k in (o, o + 1)]
        pick[o * HALF : (o + 2) * HALF, :] = jnp.concatenate(pair, axis=0).astype(jnp.bfloat16)
    r, lane = iota((32, OWNERS), 0), iota((32, OWNERS), 1)
    late = (lane == HALF + PIECE * (r // 8) + r % 8) & (r % 8 < PIECE)
    last = one_hot(late, blocks_ref[pl.ds(hot, 1), :])
    pick[OWNERS * HALF :, :] = last.astype(jnp.bfloat16)

    got = jnp.dot(pick[...], source[...], preferred_element_type=jnp.float32)

    sub, lane = iota((HALF, E), 0), iota((HALF, E), 1)
    place = lane - sub == (me % NX) * BLOCK
    sub8, lane8 = iota((8, E), 0), iota((8, E), 1)
    place8 = (lane8 - sub8 == (me % 16) * 8) & (sub8 < PIECE)
    tails = []
    for x in range(NX):
        part = got[OWNERS * HALF + 8 * x : OWNERS * HALF + 8 * x + 8]
        where_to = part[:, 2 * E : 3 * E] * 256.0 + part[:, 3 * E :] + 1.0
        row = jnp.sum(jnp.where(place8, where_to, 0.0), axis=0, keepdims=True)
        tails.append(jnp.where(sub8 < PIECE, part[:, :E] + part[:, E : 2 * E], row))
    for o in range(OWNERS):
        part = got[o * HALF : (o + 1) * HALF]
        send_ref[o, :HALF, :] = part[:, :E] + part[:, E : 2 * E]
        where_to = part[:, 2 * E : 3 * E] * 256.0 + part[:, 3 * E :] + 1.0
        used = place & (sub < counts_ref[0, o])
        row = jnp.sum(jnp.where(used, where_to, 0.0), axis=0, keepdims=True)
        send_ref[o, HALF:, :] = jnp.where(sub8 == PIECE, row, tails[o % NX])


def pack(me, counts, drow, ids, blocks):
    whole = pl.BlockSpec(memory_space=pltpu.VMEM)
    scalar = pl.BlockSpec(memory_space=pltpu.SMEM)
    return pl.pallas_call(
        pack_kernel,
        out_shape=jax.ShapeDtypeStruct((OWNERS, BLOCK, E), jnp.float32),
        in_specs=[scalar, scalar, whole, whole, whole],
        out_specs=whole,
        scratch_shapes=[
            pltpu.VMEM((OWNERS * HALF + 32, SLOTS), jnp.bfloat16),
            pltpu.VMEM((SLOTS, 4 * E), jnp.bfloat16),
        ],
        compiler_params=pltpu.CompilerParams(vmem_limit_bytes=VMEM_LIMIT),
        cost_estimate=pl.CostEstimate(
            flops=2 * 1184 * 1024 * 512, bytes_accessed=2_000_000, transcendentals=0
        ),
        name="pack",
    )(me, counts, drow, ids, blocks)


STEP = 512
NEAR = PART + OWNERS * 8


def add_kernel(me_ref, counts_ref, got_ref, near_ref, table_ref, rows, dest):
    groups = OWNERS // NX
    for g in range(groups):
        rows[g * 128 : (g + 1) * 128, :] = split(got_ref[g * 128 : (g + 1) * 128, :])
        total = sum(got_ref[(NX * g + j) * BLOCK + HALF : (NX * g + j + 1) * BLOCK, :] for j in range(NX))
        dest[:, g * 128 : (g + 1) * 128] = jnp.broadcast_to(total[PIECE : PIECE + 1, :], (8, E))

    def product(t):
        table_row = (iota((STEP, E), 0) + (t * STEP + 1)).astype(jnp.float32)
        hits = [
            jnp.where(table_row == dest[0:1, g * 128 : (g + 1) * 128], 1.0, 0.0).astype(jnp.bfloat16)
            for g in range(groups)
        ]
        both = jnp.dot(jnp.concatenate(hits, axis=1), rows[...], preferred_element_type=jnp.float32)
        return both[:, :E] + both[:, E:]

    for t in range(ROWS_DEV // STEP):
        table_ref[t * STEP : (t + 1) * STEP, :] = product(t)

    @pl.when(counts_ref[0, me_ref[0]] > HALF)
    def _():
        for k in range(NX):
            for g in range(3):
                base = k * NEAR + PART
                tiles = [near_ref[base + t * 8 : base + t * 8 + 8, :] for t in range(16 * g, 16 * g + 16)]
                at = (k * 3 + g) * 128
                rows[at : at + 128, :] = split(jnp.concatenate(tiles, axis=0))
                dest[:, at : at + 128] = jnp.broadcast_to(sum(tiles)[7:8, :], (8, E))
        for t in range(ROWS_DEV // STEP):
            table_ref[t * STEP : (t + 1) * STEP, :] += product(t)


def add_rows(me, counts, got, near):
    whole = pl.BlockSpec(memory_space=pltpu.VMEM)
    scalar = pl.BlockSpec(memory_space=pltpu.SMEM)
    return pl.pallas_call(
        add_kernel,
        out_shape=jax.ShapeDtypeStruct((ROWS_DEV, E), jnp.float32),
        in_specs=[scalar, scalar, whole, whole],
        out_specs=whole,
        scratch_shapes=[
            pltpu.VMEM((OWNERS * BLOCK, 2 * E), jnp.bfloat16),
            pltpu.VMEM((8, OWNERS * BLOCK), jnp.float32),
        ],
        compiler_params=pltpu.CompilerParams(vmem_limit_bytes=VMEM_LIMIT),
        cost_estimate=pl.CostEstimate(
            flops=2 * 2048 * 1536 * 256, bytes_accessed=2_500_000, transcendentals=0
        ),
        name="add_rows",
    )(me, counts, got, near)


SWAPS = (1, 2, 4, 14)


def grp_swap(bits):
    return [(g, g ^ bits) for g in range(16)]


X_GROUPS = [[z * NX + x for x in range(NX)] for z in range(OWNERS // NX)]
Z_GROUPS = [[z * NX + x for z in range(OWNERS // NX)] for x in range(NX)]


def join_kernel(keep_ref, there_ref, got_ref, near_ref):
    part = keep_ref[...] + there_ref[...]
    for x in range(NX):
        near_ref[x, :PART, :] = part
        for s in range(OWNERS):
            near_ref[x, PART + s * 8 : PART + s * 8 + 8, :] = got_ref[s * BLOCK + HALF : (s + 1) * BLOCK, :]


def join(keep, there, got):
    whole = pl.BlockSpec(memory_space=pltpu.VMEM)
    return pl.pallas_call(
        join_kernel,
        out_shape=jax.ShapeDtypeStruct((NX, NEAR, E), jnp.float32),
        in_specs=[whole, whole, whole],
        out_specs=whole,
        compiler_params=pltpu.CompilerParams(vmem_limit_bytes=VMEM_LIMIT),
        cost_estimate=pl.CostEstimate(flops=11264, bytes_accessed=2_000_000, transcendentals=0),
        name="join",
    )(keep, there, got)


def spread_kernel(near_ref, out_ref):
    part = near_ref[:PART, :]
    for x in range(1, NX):
        part += near_ref[x * NEAR : x * NEAR + PART, :]
    for z in range(OWNERS // NX):
        out_ref[z] = part


def spread_sum(near):
    whole = pl.BlockSpec(memory_space=pltpu.VMEM)
    return pl.pallas_call(
        spread_kernel,
        out_shape=jax.ShapeDtypeStruct((OWNERS // NX, PART, E), jnp.float32),
        in_specs=[whole],
        out_specs=whole,
        compiler_params=pltpu.CompilerParams(vmem_limit_bytes=VMEM_LIMIT),
        cost_estimate=pl.CostEstimate(flops=33792, bytes_accessed=1_500_000, transcendentals=0),
        name="spread_sum",
    )(near)


def final_kernel(g_ref, parts_ref, w1_ref, b1_ref, w2_ref, b2_ref, w3_ref):
    total = parts_ref[0]
    for z in range(1, OWNERS // NX):
        total += parts_ref[z]
    g = g_ref[0]
    w1_ref[:, :E] = total[:32]
    w1_ref[:, E:] = total[32:64]
    w2_ref[...] = total[64:80]
    small = total[80:88]
    by16 = pltpu.roll(small, (128 - (g % 8) * 16) % 128, 1)
    by8 = pltpu.roll(small, (128 - g * 8) % 128, 1)
    b1_ref[...] = jnp.where(g < 8, by16[0:1, :16], by16[1:2, :16])
    b2_ref[...] = by8[2:3, :8]
    w3_ref[...] = by8[3:4, :8]


def final(g, parts):
    whole = pl.BlockSpec(memory_space=pltpu.VMEM)
    shapes = ((32, 2 * E), (1, 16), (16, E), (1, 8), (1, 8))
    return pl.pallas_call(
        final_kernel,
        out_shape=[jax.ShapeDtypeStruct(shape, jnp.float32) for shape in shapes],
        in_specs=[pl.BlockSpec(memory_space=pltpu.SMEM), whole],
        out_specs=[whole] * 5,
        compiler_params=pltpu.CompilerParams(vmem_limit_bytes=VMEM_LIMIT),
        cost_estimate=pl.CostEstimate(flops=135168, bytes_accessed=600_000, transcendentals=0),
        name="final",
    )(g, parts)


def shards(
    target,
    history,
    lengths,
    hist_ids,
    block_rows,
    block_counts,
    attn_w1,
    attn_b1,
    attn_w2,
    attn_b2,
    attn_w3,
    pooled_gradient,
):
    g = lax.axis_index("grp")
    me = lax.axis_index("shard").reshape(1)
    drow, part = dense(
        lengths,
        target,
        history.reshape(SLOTS, E),
        pooled_gradient,
        attn_w1,
        attn_b1.reshape(1, 2 * E),
        attn_w2,
        attn_b2.reshape(1, E),
        attn_w3.reshape(1, E),
    )
    send = pack(me, block_counts, drow, hist_ids, block_rows[0])
    got = lax.all_to_all(send, "shard", split_axis=0, concat_axis=0, tiled=True)
    got = got.reshape(OWNERS * BLOCK, E)

    part = part.reshape(2, 2, 2, 2, PART, E)
    y2 = (g >> 3) & 1
    bits = (g & 1, ((g >> 1) & 1) ^ y2, ((g >> 2) & 1) ^ y2, y2)
    for bit, swap in zip(bits, SWAPS):
        keep = lax.dynamic_index_in_dim(part, bit, 0, False)
        send = lax.dynamic_index_in_dim(part, 1 - bit, 0, False)
        there = lax.ppermute(send, "grp", grp_swap(swap))
        part = join(keep, there, got) if swap == SWAPS[-1] else keep + there
    near = lax.all_to_all(
        part, "shard", split_axis=0, concat_axis=0, tiled=True, axis_index_groups=X_GROUPS
    ).reshape(NX * NEAR, E)
    parts = lax.all_to_all(
        spread_sum(near), "shard", split_axis=0, concat_axis=0, tiled=True, axis_index_groups=Z_GROUPS
    )
    table = add_rows(me, block_counts, got, near)
    grad_w1, grad_b1, grad_w2, grad_b2, grad_w3 = final(g.reshape(1), parts)
    return (
        table[None],
        grad_w1,
        grad_b1.reshape(16),
        grad_w2,
        grad_b2.reshape(8),
        grad_w3.reshape(8),
    )


def solution(mesh):
    placed = (
        P(("grp", "shard"), None),
        P(("grp", "shard"), None, None),
        P(("grp", "shard")),
        P(("grp", "shard"), None),
        P(("grp", "shard"), None, None),
        P(("grp", "shard"), None),
        P(),
        P(),
        P(),
        P(),
        P(),
        P(("grp", "shard"), None),
    )
    return jax.shard_map(
        shards,
        mesh=mesh,
        in_specs=placed,
        out_specs=(
            P("grp", "shard", None),
            P("grp", None),
            P("grp"),
            P("grp", None),
            P("grp"),
            P("grp"),
        ),
        check_vma=False,
    )
```

```python
import jax
import jax.numpy as jnp
from jax import lax
from jax.experimental import pallas as pl
from jax.experimental.pallas import tpu as pltpu
from jax.sharding import PartitionSpec as P

ROWS_DEV = 2048
E = 128
OWNERS = 48
HALF = 24
BLOCK = 32
NX = 4
PIECE = 6
SLOTS = 1024
VMEM_LIMIT = 24 * 1024 * 1024


def iota(shape, dim):
    return lax.broadcasted_iota(jnp.int32, shape, dim)


def split(rows):
    high = rows.astype(jnp.bfloat16)
    low = (rows - high.astype(jnp.float32)).astype(jnp.bfloat16)
    return jnp.concatenate([high, low], axis=1)


CHUNK = 256
QUARTER = 24
PART = NX * QUARTER


def sigmoid(z):
    return 0.5 * jnp.tanh(0.5 * z) + 0.5


def places():
    at = []
    for g in range(16):
        core, y0, y1, y2 = g & 1, (g >> 1) & 1, (g >> 2) & 1, (g >> 3) & 1
        at.append((y0 ^ y2) * 8 + core * 4 + (y1 ^ y2) * 2 + y2)
    return at


def dense_kernel(
    lengths_ref, target_in, hist_in, pg_in, w1_in, b1_in, w2_in, b2_in, w3_in,
    drow_ref, part_ref,
    target_ref, hist_ref, pg_ref, w1_ref, b1_ref, w2_ref, b2_ref, w3_ref,
    feats, act1s, dz2s, dz1s, sems,
):
    inputs = (hist_in, w1_in, target_in, b1_in, w2_in, b2_in, w3_in, pg_in)
    held = (hist_ref, w1_ref, target_ref, b1_ref, w2_ref, b2_ref, w3_ref, pg_ref)
    copies = [pltpu.make_async_copy(a, b, sems.at[k]) for k, (a, b) in enumerate(zip(inputs, held))]
    for copy in copies:
        copy.start()
    for copy in copies:
        copy.wait()
    query = target_ref[...].astype(jnp.float32)
    w1, w2, w3 = w1_ref[...], w2_ref[...], w3_ref[...]
    grad_w3 = jnp.zeros((1, E), jnp.float32)
    grad_b2 = jnp.zeros((1, E), jnp.float32)
    grad_b1 = jnp.zeros((1, 2 * E), jnp.float32)
    samples = CHUNK // 128
    across = (((1,), (1,)), ((), ()))
    down = (((0,), (0,)), ((), ()))
    for c in range(SLOTS // CHUNK):
        rows = slice(c * CHUNK, (c + 1) * CHUNK)
        hist_low = hist_ref[rows, :]
        hist = hist_low.astype(jnp.float32)
        def spread(rows_of):
            parts = [rows_of[b : b + 1, :] for b in range(c * samples, (c + 1) * samples)]
            return jnp.concatenate([jnp.broadcast_to(v, (128, E)) for v in parts], axis=0)
        q = spread(query)
        pg = spread(pg_ref)
        live = jnp.concatenate(
            [iota((128, 1), 0) < lengths_ref[b] for b in range(c * samples, (c + 1) * samples)], axis=0
        )
        feat = jnp.concatenate(
            [q.astype(jnp.bfloat16), hist_low, (q - hist).astype(jnp.bfloat16), (q * hist).astype(jnp.bfloat16)],
            axis=1,
        )
        feats[rows, :] = feat
        act1 = sigmoid(jnp.dot(feat, w1, preferred_element_type=jnp.float32) + b1_ref[...])
        act1_low = act1.astype(jnp.bfloat16)
        act1s[rows, :] = act1_low
        act2 = sigmoid(jnp.dot(act1_low, w2, preferred_element_type=jnp.float32) + b2_ref[...])
        score = jnp.where(live, jnp.sum(act2 * w3, axis=1, keepdims=True), 0.0)
        dscore = jnp.where(live, jnp.sum(pg * hist, axis=1, keepdims=True), 0.0)
        dact2 = dscore * act2
        grad_w3 += jnp.sum(dact2, axis=0, keepdims=True)
        dz2_full = dact2 * w3 * (1.0 - act2)
        grad_b2 += jnp.sum(dz2_full, axis=0, keepdims=True)
        dz2 = dz2_full.astype(jnp.bfloat16)
        dz2s[rows, :] = dz2
        back = lax.dot_general(dz2, w2, across, preferred_element_type=jnp.float32)
        dz1_full = back * act1 * (1.0 - act1)
        grad_b1 += jnp.sum(dz1_full, axis=0, keepdims=True)
        dz1 = dz1_full.astype(jnp.bfloat16)
        dz1s[rows, :] = dz1
        dfeat = lax.dot_general(dz1, w1[E:, :], across, preferred_element_type=jnp.float32)
        drow_ref[rows, :] = dfeat[:, :E] - dfeat[:, E : 2 * E] + dfeat[:, 2 * E :] * q + score * pg

    grad_w1 = lax.dot_general(feats[...], dz1s[...], down, preferred_element_type=jnp.float32)
    grad_w2 = lax.dot_general(act1s[...], dz2s[...], down, preferred_element_type=jnp.float32)
    sub = iota((8, E), 0)
    small = jnp.where(sub == 0, grad_b1[:, :E], jnp.where(sub == 1, grad_b1[:, E:], 0.0))
    small = jnp.where(sub == 2, grad_b2, jnp.where(sub == 3, grad_w3, small))
    for g, at in enumerate(places()):
        for k in range(NX):
            base = at * PART + k * QUARTER
            top = 32 * g + 16 * (k % 2)
            side = E * (k // 2)
            part_ref[base : base + 16, :] = grad_w1[top : top + 16, side : side + E]
            if k < 2:
                last = grad_w2[16 * g + 8 * k : 16 * g + 8 * k + 8, :]
            else:
                last = small
            part_ref[base + 16 : base + 24, :] = last


def dense(lengths, target, hist, pg, w1, b1, w2, b2, w3):
    whole = pl.BlockSpec(memory_space=pltpu.VMEM)
    scalar = pl.BlockSpec(memory_space=pltpu.SMEM)
    return pl.pallas_call(
        dense_kernel,
        out_shape=[
            jax.ShapeDtypeStruct((SLOTS, E), jnp.float32),
            jax.ShapeDtypeStruct((16 * PART, E), jnp.float32),
        ],
        in_specs=[scalar] + [pl.BlockSpec(memory_space=pltpu.HBM)] * 8,
        out_specs=[whole, whole],
        scratch_shapes=[pltpu.VMEM(v.shape, v.dtype) for v in (target, hist, pg, w1, b1, w2, b2, w3)]
        + [
            pltpu.VMEM((SLOTS, 4 * E), jnp.bfloat16),
            pltpu.VMEM((SLOTS, 2 * E), jnp.bfloat16),
            pltpu.VMEM((SLOTS, E), jnp.bfloat16),
            pltpu.VMEM((SLOTS, 2 * E), jnp.bfloat16),
            pltpu.SemaphoreType.DMA((8,)),
        ],
        compiler_params=pltpu.CompilerParams(vmem_limit_bytes=VMEM_LIMIT),
        cost_estimate=pl.CostEstimate(
            flops=1_100_000_000, bytes_accessed=2_200_000, transcendentals=400_000
        ),
        name="dense",
    )(lengths, target, hist, pg, w1, b1, w2, b2, w3)


def pack_kernel(
    me_ref, counts_ref, drow_ref, ids_in, blocks_in, send_ref, ids_ref, blocks_ref, pick, source, sems
):
    copies = [
        pltpu.make_async_copy(ids_in, ids_ref, sems.at[0]),
        pltpu.make_async_copy(blocks_in, blocks_ref, sems.at[1]),
    ]
    for copy in copies:
        copy.start()
    me = me_ref[0]
    hot = jnp.int32(0)
    for o in range(OWNERS):
        hot = jnp.where(counts_ref[0, o] > HALF, jnp.int32(o), hot)

    source[:, : 2 * E] = split(drow_ref[...])
    for copy in copies:
        copy.wait()
    ids = ids_ref[...] & (ROWS_DEV - 1)
    id_columns = jnp.transpose(ids.astype(jnp.float32))
    for b in range(8):
        column = jnp.broadcast_to(id_columns[:, b : b + 1], (128, 128)).astype(jnp.int32)
        source[b * 128 : (b + 1) * 128, 2 * E : 3 * E] = (column >> 8).astype(jnp.float32).astype(jnp.bfloat16)
        source[b * 128 : (b + 1) * 128, 3 * E :] = (column & 255).astype(jnp.float32).astype(jnp.bfloat16)

    slot = iota((8, SLOTS), 1).astype(jnp.float32)[:1]
    eye = iota((HALF, OWNERS), 0) == iota((HALF, OWNERS), 1)
    def one_hot(mask, row):
        chosen = jnp.where(mask, row.astype(jnp.float32), 0.0)
        column = jnp.sum(chosen, axis=1, keepdims=True)
        return jnp.where(column == slot, 1.0, 0.0)
    for o in range(0, OWNERS, 2):
        pair = [one_hot(eye, blocks_ref[k : k + 1, :]) for k in (o, o + 1)]
        pick[o * HALF : (o + 2) * HALF, :] = jnp.concatenate(pair, axis=0).astype(jnp.bfloat16)
    r, lane = iota((32, OWNERS), 0), iota((32, OWNERS), 1)
    late = (lane == HALF + PIECE * (r // 8) + r % 8) & (r % 8 < PIECE)
    last = one_hot(late, blocks_ref[pl.ds(hot, 1), :])
    pick[OWNERS * HALF :, :] = last.astype(jnp.bfloat16)

    got = jnp.dot(pick[...], source[...], preferred_element_type=jnp.float32)

    sub, lane = iota((HALF, E), 0), iota((HALF, E), 1)
    place = lane - sub == (me % NX) * BLOCK
    sub8, lane8 = iota((8, E), 0), iota((8, E), 1)
    place8 = (lane8 - sub8 == (me % 16) * 8) & (sub8 < PIECE)
    tails = []
    for x in range(NX):
        part = got[OWNERS * HALF + 8 * x : OWNERS * HALF + 8 * x + 8]
        where_to = part[:, 2 * E : 3 * E] * 256.0 + part[:, 3 * E :] + 1.0
        row = jnp.sum(jnp.where(place8, where_to, 0.0), axis=0, keepdims=True)
        tails.append(jnp.where(sub8 < PIECE, part[:, :E] + part[:, E : 2 * E], row))
    for o in range(OWNERS):
        part = got[o * HALF : (o + 1) * HALF]
        send_ref[o, :HALF, :] = part[:, :E] + part[:, E : 2 * E]
        where_to = part[:, 2 * E : 3 * E] * 256.0 + part[:, 3 * E :] + 1.0
        used = place & (sub < counts_ref[0, o])
        row = jnp.sum(jnp.where(used, where_to, 0.0), axis=0, keepdims=True)
        send_ref[o, HALF:, :] = jnp.where(sub8 == PIECE, row, tails[o % NX])


def pack(me, counts, drow, ids, blocks):
    whole = pl.BlockSpec(memory_space=pltpu.VMEM)
    scalar = pl.BlockSpec(memory_space=pltpu.SMEM)
    return pl.pallas_call(
        pack_kernel,
        out_shape=jax.ShapeDtypeStruct((OWNERS, BLOCK, E), jnp.float32),
        in_specs=[scalar, scalar, whole] + [pl.BlockSpec(memory_space=pltpu.HBM)] * 2,
        out_specs=whole,
        scratch_shapes=[
            pltpu.VMEM(ids.shape, ids.dtype),
            pltpu.VMEM(blocks.shape, blocks.dtype),
            pltpu.VMEM((OWNERS * HALF + 32, SLOTS), jnp.bfloat16),
            pltpu.VMEM((SLOTS, 4 * E), jnp.bfloat16),
            pltpu.SemaphoreType.DMA((2,)),
        ],
        compiler_params=pltpu.CompilerParams(vmem_limit_bytes=VMEM_LIMIT),
        cost_estimate=pl.CostEstimate(
            flops=2 * 1184 * 1024 * 512, bytes_accessed=2_000_000, transcendentals=0
        ),
        name="pack",
    )(me, counts, drow, ids, blocks)


STEP = 512


def add_kernel(me_ref, counts_ref, got_ref, own_ref, late0_ref, late1_ref, late2_ref, table_ref, rows, dest):
    groups = OWNERS // NX
    for g in range(groups):
        rows[g * 128 : (g + 1) * 128, :] = split(got_ref[g * 128 : (g + 1) * 128, :])
        total = sum(got_ref[(NX * g + j) * BLOCK + HALF : (NX * g + j + 1) * BLOCK, :] for j in range(NX))
        dest[:, g * 128 : (g + 1) * 128] = jnp.broadcast_to(total[PIECE : PIECE + 1, :], (8, E))

    def product(t):
        table_row = (iota((STEP, E), 0) + (t * STEP + 1)).astype(jnp.float32)
        hits = [
            jnp.where(table_row == dest[0:1, g * 128 : (g + 1) * 128], 1.0, 0.0).astype(jnp.bfloat16)
            for g in range(groups)
        ]
        both = jnp.dot(jnp.concatenate(hits, axis=1), rows[...], preferred_element_type=jnp.float32)
        return both[:, :E] + both[:, E:]

    for t in range(ROWS_DEV // STEP):
        table_ref[t * STEP : (t + 1) * STEP, :] = product(t)

    @pl.when(counts_ref[0, me_ref[0]] > HALF)
    def _():
        for k in range(NX):
            for g in range(3):
                late = (own_ref, late0_ref, late1_ref, late2_ref)[k]
                tiles = [late[t * 8 : t * 8 + 8, :] for t in range(16 * g, 16 * g + 16)]
                at = (k * 3 + g) * 128
                rows[at : at + 128, :] = split(jnp.concatenate(tiles, axis=0))
                dest[:, at : at + 128] = jnp.broadcast_to(sum(tiles)[7:8, :], (8, E))
        for t in range(ROWS_DEV // STEP):
            table_ref[t * STEP : (t + 1) * STEP, :] += product(t)


def add_rows(me, counts, got, late):
    whole = pl.BlockSpec(memory_space=pltpu.VMEM)
    scalar = pl.BlockSpec(memory_space=pltpu.SMEM)
    return pl.pallas_call(
        add_kernel,
        out_shape=jax.ShapeDtypeStruct((ROWS_DEV, E), jnp.float32),
        in_specs=[scalar, scalar] + [whole] * 5,
        out_specs=whole,
        scratch_shapes=[
            pltpu.VMEM((OWNERS * BLOCK, 2 * E), jnp.bfloat16),
            pltpu.VMEM((8, OWNERS * BLOCK), jnp.float32),
        ],
        compiler_params=pltpu.CompilerParams(vmem_limit_bytes=VMEM_LIMIT),
        cost_estimate=pl.CostEstimate(
            flops=2 * 2048 * 1536 * 256, bytes_accessed=2_500_000, transcendentals=0
        ),
        name="add_rows",
    )(me, counts, got, *late)


GRP_SWAPS = (2, 1, 4, 14)
X_SWAPS = (1, 3)
NZ = OWNERS // NX
X_GROUPS = [[z * NX + x for x in range(NX)] for z in range(NZ)]
Z_GROUPS = [[z * NX + x for z in range(NZ)] for x in range(NX)]


def swap(value, axis, bits):
    size = lax.axis_size(axis)
    return lax.ppermute(value, axis, [(i, i ^ bits) for i in range(size)])


def join_kernel(keep_ref, there_ref, got_ref, copies_ref, slab_ref):
    part = keep_ref[...] + there_ref[...]
    for z in range(NZ):
        copies_ref[z] = part
    for s in range(OWNERS):
        slab_ref[s * 8 : s * 8 + 8, :] = got_ref[s * BLOCK + HALF : (s + 1) * BLOCK, :]


def join(keep, there, got):
    whole = pl.BlockSpec(memory_space=pltpu.VMEM)
    return pl.pallas_call(
        join_kernel,
        out_shape=[
            jax.ShapeDtypeStruct((NZ, QUARTER, E), jnp.float32),
            jax.ShapeDtypeStruct((OWNERS * 8, E), jnp.float32),
        ],
        in_specs=[whole, whole, whole],
        out_specs=[whole, whole],
        compiler_params=pltpu.CompilerParams(vmem_limit_bytes=VMEM_LIMIT),
        cost_estimate=pl.CostEstimate(flops=3072, bytes_accessed=1_300_000, transcendentals=0),
        name="join",
    )(keep, there, got)


def spread_kernel(parts_ref, out_ref):
    part = parts_ref[0]
    for z in range(1, NZ):
        part += parts_ref[z]
    for x in range(NX):
        out_ref[x] = part


def spread_sum(parts):
    whole = pl.BlockSpec(memory_space=pltpu.VMEM)
    return pl.pallas_call(
        spread_kernel,
        out_shape=jax.ShapeDtypeStruct((NX, QUARTER, E), jnp.float32),
        in_specs=[whole],
        out_specs=whole,
        compiler_params=pltpu.CompilerParams(vmem_limit_bytes=VMEM_LIMIT),
        cost_estimate=pl.CostEstimate(flops=33792, bytes_accessed=200_000, transcendentals=0),
        name="spread_sum",
    )(parts)


HOLDER = (0, 3, 1, 2)


def final_kernel(g_ref, total_ref, w1_ref, b1_ref, w2_ref, b2_ref, w3_ref):
    quarters = [total_ref[x] for x in HOLDER]
    for k in range(NX):
        top, side = 16 * (k % 2), E * (k // 2)
        w1_ref[top : top + 16, side : side + E] = quarters[k][:16]
    w2_ref[:8, :] = quarters[0][16:]
    w2_ref[8:, :] = quarters[1][16:]
    g = g_ref[0]
    small = quarters[2][16:]
    by16 = pltpu.roll(small, (128 - (g % 8) * 16) % 128, 1)
    by8 = pltpu.roll(small, (128 - g * 8) % 128, 1)
    b1_ref[...] = jnp.where(g < 8, by16[0:1, :16], by16[1:2, :16])
    b2_ref[...] = by8[2:3, :8]
    w3_ref[...] = by8[3:4, :8]


def final(g, total):
    whole = pl.BlockSpec(memory_space=pltpu.VMEM)
    shapes = ((32, 2 * E), (1, 16), (16, E), (1, 8), (1, 8))
    return pl.pallas_call(
        final_kernel,
        out_shape=[jax.ShapeDtypeStruct(shape, jnp.float32) for shape in shapes],
        in_specs=[pl.BlockSpec(memory_space=pltpu.SMEM), whole],
        out_specs=[whole] * 5,
        compiler_params=pltpu.CompilerParams(vmem_limit_bytes=VMEM_LIMIT),
        cost_estimate=pl.CostEstimate(flops=1024, bytes_accessed=100_000, transcendentals=0),
        name="final",
    )(g, total)


def shards(
    target,
    history,
    lengths,
    hist_ids,
    block_rows,
    block_counts,
    attn_w1,
    attn_b1,
    attn_w2,
    attn_b2,
    attn_w3,
    pooled_gradient,
):
    g = lax.axis_index("grp")
    me = lax.axis_index("shard").reshape(1)
    drow, part = dense(
        lengths,
        target,
        history.reshape(SLOTS, E),
        pooled_gradient,
        attn_w1,
        attn_b1.reshape(1, 2 * E),
        attn_w2,
        attn_b2.reshape(1, E),
        attn_w3.reshape(1, E),
    )
    send = pack(me, block_counts, drow, hist_ids, block_rows[0])
    got = lax.all_to_all(send, "shard", split_axis=0, concat_axis=0, tiled=True)
    got = got.reshape(OWNERS * BLOCK, E)

    part = part.reshape(2, 2, 2, 2, 2, 2, QUARTER, E)
    y2 = (g >> 3) & 1
    x1 = (me[0] >> 1) & 1
    bits = (((g >> 1) & 1) ^ y2, g & 1, ((g >> 2) & 1) ^ y2, y2, (me[0] & 1) ^ x1, x1)
    steps = [("grp", k) for k in GRP_SWAPS] + [("shard", k) for k in X_SWAPS]
    for bit, (axis, k) in zip(bits, steps):
        keep = lax.dynamic_index_in_dim(part, bit, 0, False)
        away = lax.dynamic_index_in_dim(part, 1 - bit, 0, False)
        there = swap(away, axis, k)
        part = keep + there
    copies, slab = join(keep, there, got)
    parts = lax.all_to_all(
        copies, "shard", split_axis=0, concat_axis=0, tiled=True, axis_index_groups=Z_GROUPS
    )
    total = lax.all_to_all(
        spread_sum(parts), "shard", split_axis=0, concat_axis=0, tiled=True, axis_index_groups=X_GROUPS
    )
    late = [slab]
    for turn in (1, 2, 3):
        pairs = [(s, s // NX * NX + (s + turn) % NX) for s in range(OWNERS)]
        late.append(lax.ppermute(slab, "shard", pairs))
    table = add_rows(me, block_counts, got, late)
    grad_w1, grad_b1, grad_w2, grad_b2, grad_w3 = final(g.reshape(1), total)
    return (
        table[None],
        grad_w1,
        grad_b1.reshape(16),
        grad_w2,
        grad_b2.reshape(8),
        grad_w3.reshape(8),
    )


def solution(mesh):
    placed = (
        P(("grp", "shard"), None),
        P(("grp", "shard"), None, None),
        P(("grp", "shard")),
        P(("grp", "shard"), None),
        P(("grp", "shard"), None, None),
        P(("grp", "shard"), None),
        P(),
        P(),
        P(),
        P(),
        P(),
        P(("grp", "shard"), None),
    )
    return jax.shard_map(
        shards,
        mesh=mesh,
        in_specs=placed,
        out_specs=(
            P("grp", "shard", None),
            P("grp", None),
            P("grp"),
            P("grp", None),
            P("grp"),
            P("grp"),
        ),
        check_vma=False,
    )
```

```python
import jax
import jax.numpy as jnp
from jax import lax
from jax.experimental import pallas as pl
from jax.experimental.pallas import tpu as pltpu
from jax.sharding import PartitionSpec as P

ROWS_DEV = 2048
E = 128
OWNERS = 48
HALF = 24
BLOCK = 32
NX = 4
PIECE = 6
SLOTS = 1024
VMEM_LIMIT = 24 * 1024 * 1024


def in_hbm(*values):
    return [pltpu.with_memory_space_constraint(v, pltpu.HBM) for v in values]


def iota(shape, dim):
    return lax.broadcasted_iota(jnp.int32, shape, dim)


def split(rows):
    high = rows.astype(jnp.bfloat16)
    low = (rows - high.astype(jnp.float32)).astype(jnp.bfloat16)
    return jnp.concatenate([high, low], axis=1)


CHUNK = 256
QUARTER = 24
PART = NX * QUARTER


def sigmoid(z):
    return 0.5 * jnp.tanh(0.5 * z) + 0.5


def places():
    at = []
    for g in range(16):
        core, y0, y1, y2 = g & 1, (g >> 1) & 1, (g >> 2) & 1, (g >> 3) & 1
        at.append((y0 ^ y2) * 8 + core * 4 + (y1 ^ y2) * 2 + y2)
    return at


def dense_kernel(
    lengths_in, target_in, hist_in, pg_in, w1_in, b1_in, w2_in, b2_in, w3_in, ids_in, blocks_in,
    drow_ref, part_ref, ids_ref, blocks_ref,
    lengths_ref, target_ref, hist_ref, pg_ref, w1_ref, b1_ref, w2_ref, b2_ref, w3_ref,
    feats, act1s, dz2s, dz1s, sems,
):
    inputs = (hist_in, w1_in, target_in, b1_in, w2_in, b2_in, w3_in, pg_in, lengths_in, ids_in, blocks_in)
    held = (hist_ref, w1_ref, target_ref, b1_ref, w2_ref, b2_ref, w3_ref, pg_ref, lengths_ref, ids_ref, blocks_ref)
    copies = [pltpu.make_async_copy(a, b, sems.at[k]) for k, (a, b) in enumerate(zip(inputs, held))]
    for copy in copies:
        copy.start()
    for copy in copies:
        copy.wait()
    query = target_ref[...].astype(jnp.float32)
    w1, w2, w3 = w1_ref[...], w2_ref[...], w3_ref[...]
    grad_w3 = jnp.zeros((1, E), jnp.float32)
    grad_b2 = jnp.zeros((1, E), jnp.float32)
    grad_b1 = jnp.zeros((1, 2 * E), jnp.float32)
    samples = CHUNK // 128
    across = (((1,), (1,)), ((), ()))
    down = (((0,), (0,)), ((), ()))
    for c in range(SLOTS // CHUNK):
        rows = slice(c * CHUNK, (c + 1) * CHUNK)
        hist_low = hist_ref[rows, :]
        hist = hist_low.astype(jnp.float32)
        def spread(rows_of):
            parts = [rows_of[b : b + 1, :] for b in range(c * samples, (c + 1) * samples)]
            return jnp.concatenate([jnp.broadcast_to(v, (128, E)) for v in parts], axis=0)
        q = spread(query)
        pg = spread(pg_ref)
        live = jnp.concatenate(
            [iota((128, 1), 0) < lengths_ref[b] for b in range(c * samples, (c + 1) * samples)], axis=0
        )
        feat = jnp.concatenate(
            [q.astype(jnp.bfloat16), hist_low, (q - hist).astype(jnp.bfloat16), (q * hist).astype(jnp.bfloat16)],
            axis=1,
        )
        feats[rows, :] = feat
        act1 = sigmoid(jnp.dot(feat, w1, preferred_element_type=jnp.float32) + b1_ref[...])
        act1_low = act1.astype(jnp.bfloat16)
        act1s[rows, :] = act1_low
        act2 = sigmoid(jnp.dot(act1_low, w2, preferred_element_type=jnp.float32) + b2_ref[...])
        score = jnp.where(live, jnp.sum(act2 * w3, axis=1, keepdims=True), 0.0)
        dscore = jnp.where(live, jnp.sum(pg * hist, axis=1, keepdims=True), 0.0)
        dact2 = dscore * act2
        grad_w3 += jnp.sum(dact2, axis=0, keepdims=True)
        dz2_full = dact2 * w3 * (1.0 - act2)
        grad_b2 += jnp.sum(dz2_full, axis=0, keepdims=True)
        dz2 = dz2_full.astype(jnp.bfloat16)
        dz2s[rows, :] = dz2
        back = lax.dot_general(dz2, w2, across, preferred_element_type=jnp.float32)
        dz1_full = back * act1 * (1.0 - act1)
        grad_b1 += jnp.sum(dz1_full, axis=0, keepdims=True)
        dz1 = dz1_full.astype(jnp.bfloat16)
        dz1s[rows, :] = dz1
        dfeat = lax.dot_general(dz1, w1[E:, :], across, preferred_element_type=jnp.float32)
        drow_ref[rows, :] = dfeat[:, :E] - dfeat[:, E : 2 * E] + dfeat[:, 2 * E :] * q + score * pg

    grad_w1 = lax.dot_general(feats[...], dz1s[...], down, preferred_element_type=jnp.float32)
    grad_w2 = lax.dot_general(act1s[...], dz2s[...], down, preferred_element_type=jnp.float32)
    sub = iota((8, E), 0)
    small = jnp.where(sub == 0, grad_b1[:, :E], jnp.where(sub == 1, grad_b1[:, E:], 0.0))
    small = jnp.where(sub == 2, grad_b2, jnp.where(sub == 3, grad_w3, small))
    for g, at in enumerate(places()):
        for k in range(NX):
            base = at * PART + k * QUARTER
            top = 32 * g + 16 * (k % 2)
            side = E * (k // 2)
            part_ref[base : base + 16, :] = grad_w1[top : top + 16, side : side + E]
            if k < 2:
                last = grad_w2[16 * g + 8 * k : 16 * g + 8 * k + 8, :]
            else:
                last = small
            part_ref[base + 16 : base + 24, :] = last


def dense(lengths, target, hist, pg, w1, b1, w2, b2, w3, ids, blocks):
    whole = pl.BlockSpec(memory_space=pltpu.VMEM)
    return pl.pallas_call(
        dense_kernel,
        out_shape=[
            jax.ShapeDtypeStruct((SLOTS, E), jnp.float32),
            jax.ShapeDtypeStruct((16 * PART, E), jnp.float32),
            jax.ShapeDtypeStruct(ids.shape, ids.dtype),
            jax.ShapeDtypeStruct(blocks.shape, blocks.dtype),
        ],
        in_specs=[pl.BlockSpec(memory_space=pltpu.HBM)] * 11,
        out_specs=[whole] * 4,
        scratch_shapes=[pltpu.SMEM(lengths.shape, lengths.dtype)]
        + [pltpu.VMEM(v.shape, v.dtype) for v in (target, hist, pg, w1, b1, w2, b2, w3)]
        + [
            pltpu.VMEM((SLOTS, 4 * E), jnp.bfloat16),
            pltpu.VMEM((SLOTS, 2 * E), jnp.bfloat16),
            pltpu.VMEM((SLOTS, E), jnp.bfloat16),
            pltpu.VMEM((SLOTS, 2 * E), jnp.bfloat16),
            pltpu.SemaphoreType.DMA((11,)),
        ],
        compiler_params=pltpu.CompilerParams(vmem_limit_bytes=VMEM_LIMIT),
        cost_estimate=pl.CostEstimate(
            flops=1_100_000_000, bytes_accessed=2_200_000, transcendentals=400_000
        ),
        name="dense",
    )(*in_hbm(lengths, target, hist, pg, w1, b1, w2, b2, w3, ids, blocks))


def pack_kernel(
    me_ref, counts_in, drow_ref, ids_ref, blocks_ref, send_ref, counts_ref, pick, source, sem
):
    fetch = pltpu.make_async_copy(counts_in, counts_ref, sem)
    fetch.start()
    me = me_ref[0]

    source[:, : 2 * E] = split(drow_ref[...])
    ids = ids_ref[...] & (ROWS_DEV - 1)
    id_columns = jnp.transpose(ids.astype(jnp.float32))
    for b in range(8):
        column = jnp.broadcast_to(id_columns[:, b : b + 1], (128, 128)).astype(jnp.int32)
        source[b * 128 : (b + 1) * 128, 2 * E : 3 * E] = (column >> 8).astype(jnp.float32).astype(jnp.bfloat16)
        source[b * 128 : (b + 1) * 128, 3 * E :] = (column & 255).astype(jnp.float32).astype(jnp.bfloat16)

    slot = iota((8, SLOTS), 1).astype(jnp.float32)[:1]
    eye = iota((HALF, OWNERS), 0) == iota((HALF, OWNERS), 1)
    def one_hot(mask, row):
        chosen = jnp.where(mask, row.astype(jnp.float32), 0.0)
        column = jnp.sum(chosen, axis=1, keepdims=True)
        return jnp.where(column == slot, 1.0, 0.0)
    for o in range(0, OWNERS, 2):
        pair = [one_hot(eye, blocks_ref[k : k + 1, :]) for k in (o, o + 1)]
        pick[o * HALF : (o + 2) * HALF, :] = jnp.concatenate(pair, axis=0).astype(jnp.bfloat16)
    fetch.wait()
    hot = jnp.int32(0)
    for o in range(OWNERS):
        hot = jnp.where(counts_ref[0, o] > HALF, jnp.int32(o), hot)
    r, lane = iota((32, OWNERS), 0), iota((32, OWNERS), 1)
    late = (lane == HALF + PIECE * (r // 8) + r % 8) & (r % 8 < PIECE)
    last = one_hot(late, blocks_ref[pl.ds(hot, 1), :])
    pick[OWNERS * HALF :, :] = last.astype(jnp.bfloat16)

    got = jnp.dot(pick[...], source[...], preferred_element_type=jnp.float32)

    sub, lane = iota((HALF, E), 0), iota((HALF, E), 1)
    place = lane - sub == (me % NX) * BLOCK
    sub8, lane8 = iota((8, E), 0), iota((8, E), 1)
    place8 = (lane8 - sub8 == (me % 16) * 8) & (sub8 < PIECE)
    tails = []
    for x in range(NX):
        part = got[OWNERS * HALF + 8 * x : OWNERS * HALF + 8 * x + 8]
        where_to = part[:, 2 * E : 3 * E] * 256.0 + part[:, 3 * E :] + 1.0
        row = jnp.sum(jnp.where(place8, where_to, 0.0), axis=0, keepdims=True)
        tails.append(jnp.where(sub8 < PIECE, part[:, :E] + part[:, E : 2 * E], row))
    for o in range(OWNERS):
        part = got[o * HALF : (o + 1) * HALF]
        send_ref[o, :HALF, :] = part[:, :E] + part[:, E : 2 * E]
        where_to = part[:, 2 * E : 3 * E] * 256.0 + part[:, 3 * E :] + 1.0
        used = place & (sub < counts_ref[0, o])
        row = jnp.sum(jnp.where(used, where_to, 0.0), axis=0, keepdims=True)
        send_ref[o, HALF:, :] = jnp.where(sub8 == PIECE, row, tails[o % NX])


def pack(me, counts, drow, ids, blocks):
    whole = pl.BlockSpec(memory_space=pltpu.VMEM)
    scalar = pl.BlockSpec(memory_space=pltpu.SMEM)
    return pl.pallas_call(
        pack_kernel,
        out_shape=jax.ShapeDtypeStruct((OWNERS, BLOCK, E), jnp.float32),
        in_specs=[scalar, pl.BlockSpec(memory_space=pltpu.HBM), whole, whole, whole],
        out_specs=whole,
        scratch_shapes=[
            pltpu.SMEM(counts.shape, counts.dtype),
            pltpu.VMEM((OWNERS * HALF + 32, SLOTS), jnp.bfloat16),
            pltpu.VMEM((SLOTS, 4 * E), jnp.bfloat16),
            pltpu.SemaphoreType.DMA(()),
        ],
        compiler_params=pltpu.CompilerParams(vmem_limit_bytes=VMEM_LIMIT),
        cost_estimate=pl.CostEstimate(
            flops=2 * 1184 * 1024 * 512, bytes_accessed=2_000_000, transcendentals=0
        ),
        name="pack",
    )(me, *in_hbm(counts), drow, ids, blocks)


STEP = 512


def add_kernel(me_ref, counts_ref, got_ref, own_ref, late0_ref, late1_ref, late2_ref, table_ref, rows, dest):
    groups = OWNERS // NX
    for g in range(groups):
        rows[g * 128 : (g + 1) * 128, :] = split(got_ref[g * 128 : (g + 1) * 128, :])
        total = sum(got_ref[(NX * g + j) * BLOCK + HALF : (NX * g + j + 1) * BLOCK, :] for j in range(NX))
        dest[:, g * 128 : (g + 1) * 128] = jnp.broadcast_to(total[PIECE : PIECE + 1, :], (8, E))

    def product(t):
        table_row = (iota((STEP, E), 0) + (t * STEP + 1)).astype(jnp.float32)
        hits = [
            jnp.where(table_row == dest[0:1, g * 128 : (g + 1) * 128], 1.0, 0.0).astype(jnp.bfloat16)
            for g in range(groups)
        ]
        both = jnp.dot(jnp.concatenate(hits, axis=1), rows[...], preferred_element_type=jnp.float32)
        return both[:, :E] + both[:, E:]

    for t in range(ROWS_DEV // STEP):
        table_ref[t * STEP : (t + 1) * STEP, :] = product(t)

    @pl.when(counts_ref[0, me_ref[0]] > HALF)
    def _():
        for k in range(NX):
            for g in range(3):
                late = (own_ref, late0_ref, late1_ref, late2_ref)[k]
                tiles = [late[t * 8 : t * 8 + 8, :] for t in range(16 * g, 16 * g + 16)]
                at = (k * 3 + g) * 128
                rows[at : at + 128, :] = split(jnp.concatenate(tiles, axis=0))
                dest[:, at : at + 128] = jnp.broadcast_to(sum(tiles)[7:8, :], (8, E))
        for t in range(ROWS_DEV // STEP):
            table_ref[t * STEP : (t + 1) * STEP, :] += product(t)


def add_rows(me, counts, got, late):
    whole = pl.BlockSpec(memory_space=pltpu.VMEM)
    scalar = pl.BlockSpec(memory_space=pltpu.SMEM)
    return pl.pallas_call(
        add_kernel,
        out_shape=jax.ShapeDtypeStruct((ROWS_DEV, E), jnp.float32),
        in_specs=[scalar, scalar] + [whole] * 5,
        out_specs=whole,
        scratch_shapes=[
            pltpu.VMEM((OWNERS * BLOCK, 2 * E), jnp.bfloat16),
            pltpu.VMEM((8, OWNERS * BLOCK), jnp.float32),
        ],
        compiler_params=pltpu.CompilerParams(vmem_limit_bytes=VMEM_LIMIT),
        cost_estimate=pl.CostEstimate(
            flops=2 * 2048 * 1536 * 256, bytes_accessed=2_500_000, transcendentals=0
        ),
        name="add_rows",
    )(me, counts, got, *late)


GRP_SWAPS = (2, 1, 4, 14)
SIDE = 2 * QUARTER
NZ = OWNERS // NX
Z_GROUPS = [[z * NX + x for z in range(NZ)] for x in range(NX)]


def swap(value, axis, bits):
    size = lax.axis_size(axis)
    return lax.ppermute(value, axis, [(i, i ^ bits) for i in range(size)])


def join_kernel(keep_ref, there_ref, got_ref, copies_ref, slab_ref):
    part = keep_ref[...] + there_ref[...]
    for z in range(NZ):
        copies_ref[z] = part
    for s in range(OWNERS):
        slab_ref[s * 8 : s * 8 + 8, :] = got_ref[s * BLOCK + HALF : (s + 1) * BLOCK, :]


def join(keep, there, got):
    whole = pl.BlockSpec(memory_space=pltpu.VMEM)
    return pl.pallas_call(
        join_kernel,
        out_shape=[
            jax.ShapeDtypeStruct((NZ, SIDE, E), jnp.float32),
            jax.ShapeDtypeStruct((OWNERS * 8, E), jnp.float32),
        ],
        in_specs=[whole, whole, whole],
        out_specs=[whole, whole],
        compiler_params=pltpu.CompilerParams(vmem_limit_bytes=VMEM_LIMIT),
        cost_estimate=pl.CostEstimate(flops=3072, bytes_accessed=1_300_000, transcendentals=0),
        name="join",
    )(keep, there, got)


def add_kernel_z(parts_ref, out_ref):
    part = parts_ref[0]
    for z in range(1, NZ):
        part += parts_ref[z]
    out_ref[...] = part


def add_parts(parts):
    whole = pl.BlockSpec(memory_space=pltpu.VMEM)
    return pl.pallas_call(
        add_kernel_z,
        out_shape=jax.ShapeDtypeStruct((SIDE, E), jnp.float32),
        in_specs=[whole],
        out_specs=whole,
        compiler_params=pltpu.CompilerParams(vmem_limit_bytes=VMEM_LIMIT),
        cost_estimate=pl.CostEstimate(flops=67584, bytes_accessed=320_000, transcendentals=0),
        name="add_parts",
    )(parts)


def final_kernel(place_ref, mine_ref, other_ref, w1_ref, b1_ref, w2_ref, b2_ref, w3_ref):
    g, first = place_ref[0], place_ref[1] == 0
    mine, other = mine_ref[...], other_ref[...]
    low, high = jnp.where(first, mine, other), jnp.where(first, other, mine)
    quarters = [low[:QUARTER], low[QUARTER:], high[:QUARTER], high[QUARTER:]]
    for k in range(NX):
        top, side = 16 * (k % 2), E * (k // 2)
        w1_ref[top : top + 16, side : side + E] = quarters[k][:16]
    w2_ref[:8, :] = quarters[0][16:]
    w2_ref[8:, :] = quarters[1][16:]
    small = quarters[2][16:]
    by16 = pltpu.roll(small, (128 - (g % 8) * 16) % 128, 1)
    by8 = pltpu.roll(small, (128 - g * 8) % 128, 1)
    b1_ref[...] = jnp.where(g < 8, by16[0:1, :16], by16[1:2, :16])
    b2_ref[...] = by8[2:3, :8]
    w3_ref[...] = by8[3:4, :8]


def final(place, mine, other):
    whole = pl.BlockSpec(memory_space=pltpu.VMEM)
    shapes = ((32, 2 * E), (1, 16), (16, E), (1, 8), (1, 8))
    return pl.pallas_call(
        final_kernel,
        out_shape=[jax.ShapeDtypeStruct(shape, jnp.float32) for shape in shapes],
        in_specs=[pl.BlockSpec(memory_space=pltpu.SMEM), whole, whole],
        out_specs=[whole] * 5,
        compiler_params=pltpu.CompilerParams(vmem_limit_bytes=VMEM_LIMIT),
        cost_estimate=pl.CostEstimate(flops=1024, bytes_accessed=100_000, transcendentals=0),
        name="final",
    )(place, mine, other)


def shards(
    target,
    history,
    lengths,
    hist_ids,
    block_rows,
    block_counts,
    attn_w1,
    attn_b1,
    attn_w2,
    attn_b2,
    attn_w3,
    pooled_gradient,
):
    g = lax.axis_index("grp")
    me = lax.axis_index("shard").reshape(1)
    drow, part, ids, blocks = dense(
        lengths,
        target,
        history.reshape(SLOTS, E),
        pooled_gradient,
        attn_w1,
        attn_b1.reshape(1, 2 * E),
        attn_w2,
        attn_b2.reshape(1, E),
        attn_w3.reshape(1, E),
        hist_ids,
        block_rows[0],
    )
    send = pack(me, block_counts, drow, ids, blocks)
    got = lax.all_to_all(send, "shard", split_axis=0, concat_axis=0, tiled=True)
    got = got.reshape(OWNERS * BLOCK, E)

    part = part.reshape(2, 2, 2, 2, 2, SIDE, E)
    y2 = (g >> 3) & 1
    side = (me[0] ^ (me[0] >> 1)) & 1
    bits = (((g >> 1) & 1) ^ y2, g & 1, ((g >> 2) & 1) ^ y2, y2, side)
    for bit, (axis, k) in zip(bits, [("grp", k) for k in GRP_SWAPS] + [("shard", 1)]):
        keep = lax.dynamic_index_in_dim(part, bit, 0, False)
        away = lax.dynamic_index_in_dim(part, 1 - bit, 0, False)
        part = keep + swap(away, axis, k)
    copies, slab = join(part, swap(part, "shard", 3), got)
    parts = lax.all_to_all(
        copies, "shard", split_axis=0, concat_axis=0, tiled=True, axis_index_groups=Z_GROUPS
    )
    total = add_parts(parts)
    other = swap(total, "shard", 1)
    late = [slab]
    for turn in (1, 2, 3):
        pairs = [(s, s // NX * NX + (s + turn) % NX) for s in range(OWNERS)]
        late.append(lax.ppermute(slab, "shard", pairs))
    table = add_rows(me, block_counts, got, late)
    grad_w1, grad_b1, grad_w2, grad_b2, grad_w3 = final(jnp.stack([g, side]), total, other)
    return (
        table[None],
        grad_w1,
        grad_b1.reshape(16),
        grad_w2,
        grad_b2.reshape(8),
        grad_w3.reshape(8),
    )


def solution(mesh):
    placed = (
        P(("grp", "shard"), None),
        P(("grp", "shard"), None, None),
        P(("grp", "shard")),
        P(("grp", "shard"), None),
        P(("grp", "shard"), None, None),
        P(("grp", "shard"), None),
        P(),
        P(),
        P(),
        P(),
        P(),
        P(("grp", "shard"), None),
    )
    return jax.shard_map(
        shards,
        mesh=mesh,
        in_specs=placed,
        out_specs=(
            P("grp", "shard", None),
            P("grp", None),
            P("grp"),
            P("grp", None),
            P("grp"),
            P("grp"),
        ),
        check_vma=False,
    )
```

```python
import jax
import jax.numpy as jnp
from jax import lax
from jax.experimental import pallas as pl
from jax.experimental.pallas import tpu as pltpu
from jax.sharding import PartitionSpec as P

ROWS_DEV = 2048
E = 128
OWNERS = 48
HALF = 24
BLOCK = 32
NX = 4
PIECE = 6
SLOTS = 1024
VMEM_LIMIT = 24 * 1024 * 1024


def in_hbm(*values):
    return [pltpu.with_memory_space_constraint(v, pltpu.HBM) for v in values]


def iota(shape, dim):
    return lax.broadcasted_iota(jnp.int32, shape, dim)


def split(rows):
    high = rows.astype(jnp.bfloat16)
    low = (rows - high.astype(jnp.float32)).astype(jnp.bfloat16)
    return jnp.concatenate([high, low], axis=1)


CHUNK = 512
QUARTER = 24
PART = NX * QUARTER


def sigmoid(z):
    return 0.5 * jnp.tanh(0.5 * z) + 0.5


def places():
    at = []
    for g in range(16):
        core, y0, y1, y2 = g & 1, (g >> 1) & 1, (g >> 2) & 1, (g >> 3) & 1
        at.append((y0 ^ y2) * 8 + core * 4 + (y1 ^ y2) * 2 + y2)
    return at


def dense_kernel(
    lengths_in, target_in, hist_in, pg_in, w1_in, b1_in, w2_in, b2_in, w3_in, ids_in, blocks_in,
    drow_ref, part_ref, ids_ref, blocks_ref,
    lengths_ref, target_ref, hist_ref, pg_ref, w1_ref, b1_ref, w2_ref, b2_ref, w3_ref,
    feats, act1s, dz2s, dz1s, sems,
):
    inputs = (hist_in, w1_in, target_in, b1_in, w2_in, b2_in, w3_in, pg_in, lengths_in, ids_in, blocks_in)
    held = (hist_ref, w1_ref, target_ref, b1_ref, w2_ref, b2_ref, w3_ref, pg_ref, lengths_ref, ids_ref, blocks_ref)
    copies = [pltpu.make_async_copy(a, b, sems.at[k]) for k, (a, b) in enumerate(zip(inputs, held))]
    for copy in copies:
        copy.start()
    for copy in copies:
        copy.wait()
    query = target_ref[...].astype(jnp.float32)
    w1, w2, w3 = w1_ref[...], w2_ref[...], w3_ref[...]
    grad_w3 = jnp.zeros((1, E), jnp.float32)
    grad_b2 = jnp.zeros((1, E), jnp.float32)
    grad_b1 = jnp.zeros((1, 2 * E), jnp.float32)
    samples = CHUNK // 128
    across = (((1,), (1,)), ((), ()))
    down = (((0,), (0,)), ((), ()))
    for c in range(SLOTS // CHUNK):
        rows = slice(c * CHUNK, (c + 1) * CHUNK)
        hist_low = hist_ref[rows, :]
        hist = hist_low.astype(jnp.float32)
        def spread(rows_of):
            parts = [rows_of[b : b + 1, :] for b in range(c * samples, (c + 1) * samples)]
            return jnp.concatenate([jnp.broadcast_to(v, (128, E)) for v in parts], axis=0)
        q = spread(query)
        pg = spread(pg_ref)
        live = jnp.concatenate(
            [iota((128, 1), 0) < lengths_ref[b] for b in range(c * samples, (c + 1) * samples)], axis=0
        )
        feat = jnp.concatenate(
            [q.astype(jnp.bfloat16), hist_low, (q - hist).astype(jnp.bfloat16), (q * hist).astype(jnp.bfloat16)],
            axis=1,
        )
        feats[rows, :] = feat
        act1 = sigmoid(jnp.dot(feat, w1, preferred_element_type=jnp.float32) + b1_ref[...])
        act1_low = act1.astype(jnp.bfloat16)
        act1s[rows, :] = act1_low
        act2 = sigmoid(jnp.dot(act1_low, w2, preferred_element_type=jnp.float32) + b2_ref[...])
        score = jnp.where(live, jnp.sum(act2 * w3, axis=1, keepdims=True), 0.0)
        dscore = jnp.where(live, jnp.sum(pg * hist, axis=1, keepdims=True), 0.0)
        dact2 = dscore * act2
        grad_w3 += jnp.sum(dact2, axis=0, keepdims=True)
        dz2_full = dact2 * w3 * (1.0 - act2)
        grad_b2 += jnp.sum(dz2_full, axis=0, keepdims=True)
        dz2 = dz2_full.astype(jnp.bfloat16)
        dz2s[rows, :] = dz2
        back = lax.dot_general(dz2, w2, across, preferred_element_type=jnp.float32)
        dz1_full = back * act1 * (1.0 - act1)
        grad_b1 += jnp.sum(dz1_full, axis=0, keepdims=True)
        dz1 = dz1_full.astype(jnp.bfloat16)
        dz1s[rows, :] = dz1
        dfeat = lax.dot_general(dz1, w1[E:, :], across, preferred_element_type=jnp.float32)
        drow_ref[rows, :] = dfeat[:, :E] - dfeat[:, E : 2 * E] + dfeat[:, 2 * E :] * q + score * pg

    grad_w1 = lax.dot_general(feats[...], dz1s[...], down, preferred_element_type=jnp.float32)
    grad_w2 = lax.dot_general(act1s[...], dz2s[...], down, preferred_element_type=jnp.float32)
    sub = iota((8, E), 0)
    small = jnp.where(sub == 0, grad_b1[:, :E], jnp.where(sub == 1, grad_b1[:, E:], 0.0))
    small = jnp.where(sub == 2, grad_b2, jnp.where(sub == 3, grad_w3, small))
    for g, at in enumerate(places()):
        for k in range(NX):
            base = at * PART + k * QUARTER
            top = 32 * g + 16 * (k % 2)
            side = E * (k // 2)
            part_ref[base : base + 16, :] = grad_w1[top : top + 16, side : side + E]
            if k < 2:
                last = grad_w2[16 * g + 8 * k : 16 * g + 8 * k + 8, :]
            else:
                last = small
            part_ref[base + 16 : base + 24, :] = last


def dense(lengths, target, hist, pg, w1, b1, w2, b2, w3, ids, blocks):
    whole = pl.BlockSpec(memory_space=pltpu.VMEM)
    return pl.pallas_call(
        dense_kernel,
        out_shape=[
            jax.ShapeDtypeStruct((SLOTS, E), jnp.float32),
            jax.ShapeDtypeStruct((16 * PART, E), jnp.float32),
            jax.ShapeDtypeStruct(ids.shape, ids.dtype),
            jax.ShapeDtypeStruct(blocks.shape, blocks.dtype),
        ],
        in_specs=[pl.BlockSpec(memory_space=pltpu.HBM)] * 11,
        out_specs=[whole] * 4,
        scratch_shapes=[pltpu.SMEM(lengths.shape, lengths.dtype)]
        + [pltpu.VMEM(v.shape, v.dtype) for v in (target, hist, pg, w1, b1, w2, b2, w3)]
        + [
            pltpu.VMEM((SLOTS, 4 * E), jnp.bfloat16),
            pltpu.VMEM((SLOTS, 2 * E), jnp.bfloat16),
            pltpu.VMEM((SLOTS, E), jnp.bfloat16),
            pltpu.VMEM((SLOTS, 2 * E), jnp.bfloat16),
            pltpu.SemaphoreType.DMA((11,)),
        ],
        compiler_params=pltpu.CompilerParams(vmem_limit_bytes=VMEM_LIMIT),
        cost_estimate=pl.CostEstimate(
            flops=1_100_000_000, bytes_accessed=2_200_000, transcendentals=400_000
        ),
        name="dense",
    )(*in_hbm(lengths, target, hist, pg, w1, b1, w2, b2, w3, ids, blocks))


def pack_kernel(
    me_ref, counts_in, drow_ref, ids_ref, blocks_ref, send_ref, counts_ref, pick, source, sem
):
    fetch = pltpu.make_async_copy(counts_in, counts_ref, sem)
    fetch.start()
    me = me_ref[0]

    source[:, : 2 * E] = split(drow_ref[...])
    ids = ids_ref[...] & (ROWS_DEV - 1)
    id_columns = jnp.transpose(ids.astype(jnp.float32))
    for b in range(8):
        column = jnp.broadcast_to(id_columns[:, b : b + 1], (128, 128)).astype(jnp.int32)
        source[b * 128 : (b + 1) * 128, 2 * E : 3 * E] = (column >> 8).astype(jnp.float32).astype(jnp.bfloat16)
        source[b * 128 : (b + 1) * 128, 3 * E :] = (column & 255).astype(jnp.float32).astype(jnp.bfloat16)

    slot = iota((8, SLOTS), 1).astype(jnp.float32)[:1]
    eye = iota((HALF, OWNERS), 0) == iota((HALF, OWNERS), 1)
    def one_hot(mask, row):
        chosen = jnp.where(mask, row.astype(jnp.float32), 0.0)
        column = jnp.sum(chosen, axis=1, keepdims=True)
        return jnp.where(column == slot, 1.0, 0.0)
    for o in range(0, OWNERS, 2):
        pair = [one_hot(eye, blocks_ref[k : k + 1, :]) for k in (o, o + 1)]
        pick[o * HALF : (o + 2) * HALF, :] = jnp.concatenate(pair, axis=0).astype(jnp.bfloat16)
    fetch.wait()
    hot = jnp.int32(0)
    for o in range(OWNERS):
        hot = jnp.where(counts_ref[0, o] > HALF, jnp.int32(o), hot)
    r, lane = iota((32, OWNERS), 0), iota((32, OWNERS), 1)
    late = (lane == HALF + PIECE * (r // 8) + r % 8) & (r % 8 < PIECE)
    last = one_hot(late, blocks_ref[pl.ds(hot, 1), :])
    pick[OWNERS * HALF :, :] = last.astype(jnp.bfloat16)

    got = jnp.dot(pick[...], source[...], preferred_element_type=jnp.float32)

    sub, lane = iota((HALF, E), 0), iota((HALF, E), 1)
    place = lane - sub == (me % NX) * BLOCK
    sub8, lane8 = iota((8, E), 0), iota((8, E), 1)
    place8 = (lane8 - sub8 == (me % 16) * 8) & (sub8 < PIECE)
    tails = []
    for x in range(NX):
        part = got[OWNERS * HALF + 8 * x : OWNERS * HALF + 8 * x + 8]
        where_to = part[:, 2 * E : 3 * E] * 256.0 + part[:, 3 * E :] + 1.0
        row = jnp.sum(jnp.where(place8, where_to, 0.0), axis=0, keepdims=True)
        tails.append(jnp.where(sub8 < PIECE, part[:, :E] + part[:, E : 2 * E], row))
    for o in range(OWNERS):
        part = got[o * HALF : (o + 1) * HALF]
        send_ref[o, :HALF, :] = part[:, :E] + part[:, E : 2 * E]
        where_to = part[:, 2 * E : 3 * E] * 256.0 + part[:, 3 * E :] + 1.0
        used = place & (sub < counts_ref[0, o])
        row = jnp.sum(jnp.where(used, where_to, 0.0), axis=0, keepdims=True)
        send_ref[o, HALF:, :] = jnp.where(sub8 == PIECE, row, tails[o % NX])


def pack(me, counts, drow, ids, blocks):
    whole = pl.BlockSpec(memory_space=pltpu.VMEM)
    scalar = pl.BlockSpec(memory_space=pltpu.SMEM)
    return pl.pallas_call(
        pack_kernel,
        out_shape=jax.ShapeDtypeStruct((OWNERS, BLOCK, E), jnp.float32),
        in_specs=[scalar, pl.BlockSpec(memory_space=pltpu.HBM), whole, whole, whole],
        out_specs=whole,
        scratch_shapes=[
            pltpu.SMEM(counts.shape, counts.dtype),
            pltpu.VMEM((OWNERS * HALF + 32, SLOTS), jnp.bfloat16),
            pltpu.VMEM((SLOTS, 4 * E), jnp.bfloat16),
            pltpu.SemaphoreType.DMA(()),
        ],
        compiler_params=pltpu.CompilerParams(vmem_limit_bytes=VMEM_LIMIT),
        cost_estimate=pl.CostEstimate(
            flops=2 * 1184 * 1024 * 512, bytes_accessed=2_000_000, transcendentals=0
        ),
        name="pack",
    )(me, *in_hbm(counts), drow, ids, blocks)


STEP = 512


def product(t, dest, rows):
    table_row = (iota((STEP, E), 0) + (t * STEP + 1)).astype(jnp.float32)
    hits = [
        jnp.where(table_row == dest[0:1, k : k + 128], 1.0, 0.0).astype(jnp.bfloat16)
        for k in range(0, OWNERS * BLOCK, 128)
    ]
    both = jnp.dot(jnp.concatenate(hits, axis=1), rows[...], preferred_element_type=jnp.float32)
    return both[:, :E] + both[:, E:]


SCATTER_SCRATCH = [
    pltpu.VMEM((OWNERS * BLOCK, 2 * E), jnp.bfloat16),
    pltpu.VMEM((8, OWNERS * BLOCK), jnp.float32),
]
SCATTER_COST = pl.CostEstimate(flops=2 * 2048 * 1536 * 256, bytes_accessed=2_500_000, transcendentals=0)


def add_main_kernel(got_ref, table_ref, rows, dest):
    for g in range(OWNERS // NX):
        rows[g * 128 : (g + 1) * 128, :] = split(got_ref[g * 128 : (g + 1) * 128, :])
        total = sum(got_ref[(NX * g + j) * BLOCK + HALF : (NX * g + j + 1) * BLOCK, :] for j in range(NX))
        dest[:, g * 128 : (g + 1) * 128] = jnp.broadcast_to(total[PIECE : PIECE + 1, :], (8, E))
    for t in range(ROWS_DEV // STEP):
        table_ref[t * STEP : (t + 1) * STEP, :] = product(t, dest, rows)


def add_main(got):
    whole = pl.BlockSpec(memory_space=pltpu.VMEM)
    return pl.pallas_call(
        add_main_kernel,
        out_shape=jax.ShapeDtypeStruct((ROWS_DEV, E), jnp.float32),
        in_specs=[whole],
        out_specs=whole,
        scratch_shapes=SCATTER_SCRATCH,
        compiler_params=pltpu.CompilerParams(vmem_limit_bytes=VMEM_LIMIT),
        cost_estimate=SCATTER_COST,
        name="add_main",
    )(got)


def add_late_kernel(
    me_ref, counts_ref, table_in, own_in, late0_in, late1_in, late2_in, table_out,
    table, late, rows, dest, sems,
):
    @pl.when(counts_ref[0, me_ref[0]] > HALF)
    def _():
        slabs = (own_in, late0_in, late1_in, late2_in)
        fetches = [pltpu.make_async_copy(slabs[k], late.at[k], sems.at[k]) for k in range(NX)]
        fetches.append(pltpu.make_async_copy(table_in, table, sems.at[NX]))
        for fetch in fetches:
            fetch.start()
        for fetch in fetches:
            fetch.wait()
        for k in range(NX):
            for g in range(3):
                tiles = [late[k, s * 8 : s * 8 + 8, :] for s in range(16 * g, 16 * g + 16)]
                at = (k * 3 + g) * 128
                rows[at : at + 128, :] = split(jnp.concatenate(tiles, axis=0))
                dest[:, at : at + 128] = jnp.broadcast_to(sum(tiles)[7:8, :], (8, E))
        for t in range(ROWS_DEV // STEP):
            table[t * STEP : (t + 1) * STEP, :] += product(t, dest, rows)
        write = pltpu.make_async_copy(table, table_out, sems.at[NX])
        write.start()
        write.wait()


def add_late(me, counts, table, late):
    scalar = pl.BlockSpec(memory_space=pltpu.SMEM)
    anywhere = pl.BlockSpec(memory_space=pl.ANY)
    return pl.pallas_call(
        add_late_kernel,
        out_shape=jax.ShapeDtypeStruct((ROWS_DEV, E), jnp.float32),
        in_specs=[scalar, scalar] + [anywhere] * 5,
        out_specs=anywhere,
        scratch_shapes=[
            pltpu.VMEM((ROWS_DEV, E), jnp.float32),
            pltpu.VMEM((NX, OWNERS * 8, E), jnp.float32),
        ]
        + SCATTER_SCRATCH
        + [pltpu.SemaphoreType.DMA((NX + 1,))],
        input_output_aliases={2: 0},
        compiler_params=pltpu.CompilerParams(vmem_limit_bytes=VMEM_LIMIT),
        cost_estimate=SCATTER_COST,
        name="add_late",
    )(me, counts, table, *late)


GRP_SWAPS = (2, 1, 4, 14)
SIDE = 2 * QUARTER
NZ = OWNERS // NX
Z_GROUPS = [[z * NX + x for z in range(NZ)] for x in range(NX)]


def swap(value, axis, bits):
    size = lax.axis_size(axis)
    return lax.ppermute(value, axis, [(i, i ^ bits) for i in range(size)])


def join_kernel(keep_ref, there_ref, got_ref, copies_ref, slab_ref):
    part = keep_ref[...] + there_ref[...]
    for z in range(NZ):
        copies_ref[z] = part
    for s in range(OWNERS):
        slab_ref[s * 8 : s * 8 + 8, :] = got_ref[s * BLOCK + HALF : (s + 1) * BLOCK, :]


def join(keep, there, got):
    whole = pl.BlockSpec(memory_space=pltpu.VMEM)
    return pl.pallas_call(
        join_kernel,
        out_shape=[
            jax.ShapeDtypeStruct((NZ, SIDE, E), jnp.float32),
            jax.ShapeDtypeStruct((OWNERS * 8, E), jnp.float32),
        ],
        in_specs=[whole, whole, whole],
        out_specs=[whole, whole],
        compiler_params=pltpu.CompilerParams(vmem_limit_bytes=VMEM_LIMIT),
        cost_estimate=pl.CostEstimate(flops=3072, bytes_accessed=1_300_000, transcendentals=0),
        name="join",
    )(keep, there, got)


def add_kernel_z(parts_ref, out_ref):
    part = parts_ref[0]
    for z in range(1, NZ):
        part += parts_ref[z]
    out_ref[...] = part


def add_parts(parts):
    whole = pl.BlockSpec(memory_space=pltpu.VMEM)
    return pl.pallas_call(
        add_kernel_z,
        out_shape=jax.ShapeDtypeStruct((SIDE, E), jnp.float32),
        in_specs=[whole],
        out_specs=whole,
        compiler_params=pltpu.CompilerParams(vmem_limit_bytes=VMEM_LIMIT),
        cost_estimate=pl.CostEstimate(flops=67584, bytes_accessed=320_000, transcendentals=0),
        name="add_parts",
    )(parts)


def final_kernel(place_ref, mine_ref, other_ref, w1_ref, b1_ref, w2_ref, b2_ref, w3_ref):
    g, first = place_ref[0], place_ref[1] == 0
    mine, other = mine_ref[...], other_ref[...]
    low, high = jnp.where(first, mine, other), jnp.where(first, other, mine)
    quarters = [low[:QUARTER], low[QUARTER:], high[:QUARTER], high[QUARTER:]]
    for k in range(NX):
        top, side = 16 * (k % 2), E * (k // 2)
        w1_ref[top : top + 16, side : side + E] = quarters[k][:16]
    w2_ref[:8, :] = quarters[0][16:]
    w2_ref[8:, :] = quarters[1][16:]
    small = quarters[2][16:]
    by16 = pltpu.roll(small, (128 - (g % 8) * 16) % 128, 1)
    by8 = pltpu.roll(small, (128 - g * 8) % 128, 1)
    b1_ref[...] = jnp.where(g < 8, by16[0:1, :16], by16[1:2, :16])
    b2_ref[...] = by8[2:3, :8]
    w3_ref[...] = by8[3:4, :8]


def final(place, mine, other):
    whole = pl.BlockSpec(memory_space=pltpu.VMEM)
    shapes = ((32, 2 * E), (1, 16), (16, E), (1, 8), (1, 8))
    return pl.pallas_call(
        final_kernel,
        out_shape=[jax.ShapeDtypeStruct(shape, jnp.float32) for shape in shapes],
        in_specs=[pl.BlockSpec(memory_space=pltpu.SMEM), whole, whole],
        out_specs=[whole] * 5,
        compiler_params=pltpu.CompilerParams(vmem_limit_bytes=VMEM_LIMIT),
        cost_estimate=pl.CostEstimate(flops=1024, bytes_accessed=100_000, transcendentals=0),
        name="final",
    )(place, mine, other)


def shards(
    target,
    history,
    lengths,
    hist_ids,
    block_rows,
    block_counts,
    attn_w1,
    attn_b1,
    attn_w2,
    attn_b2,
    attn_w3,
    pooled_gradient,
):
    g = lax.axis_index("grp")
    me = lax.axis_index("shard").reshape(1)
    drow, part, ids, blocks = dense(
        lengths,
        target,
        history.reshape(SLOTS, E),
        pooled_gradient,
        attn_w1,
        attn_b1.reshape(1, 2 * E),
        attn_w2,
        attn_b2.reshape(1, E),
        attn_w3.reshape(1, E),
        hist_ids,
        block_rows[0],
    )
    send = pack(me, block_counts, drow, ids, blocks)
    got = lax.all_to_all(send, "shard", split_axis=0, concat_axis=0, tiled=True)
    got = got.reshape(OWNERS * BLOCK, E)

    part = part.reshape(2, 2, 2, 2, 2, SIDE, E)
    y2 = (g >> 3) & 1
    side = (me[0] ^ (me[0] >> 1)) & 1
    bits = (((g >> 1) & 1) ^ y2, g & 1, ((g >> 2) & 1) ^ y2, y2, side)
    for bit, (axis, k) in zip(bits, [("grp", k) for k in GRP_SWAPS] + [("shard", 1)]):
        keep = lax.dynamic_index_in_dim(part, bit, 0, False)
        away = lax.dynamic_index_in_dim(part, 1 - bit, 0, False)
        part = keep + swap(away, axis, k)
    copies, slab = join(part, swap(part, "shard", 3), got)
    parts = lax.all_to_all(
        copies, "shard", split_axis=0, concat_axis=0, tiled=True, axis_index_groups=Z_GROUPS
    )
    total = add_parts(parts)
    other = swap(total, "shard", 1)
    late = [slab]
    for turn in (1, 2, 3):
        pairs = [(s, s // NX * NX + (s + turn) % NX) for s in range(OWNERS)]
        late.append(lax.ppermute(slab, "shard", pairs))
    table = add_late(me, block_counts, add_main(got), late)
    grad_w1, grad_b1, grad_w2, grad_b2, grad_w3 = final(jnp.stack([g, side]), total, other)
    return (
        table[None],
        grad_w1,
        grad_b1.reshape(16),
        grad_w2,
        grad_b2.reshape(8),
        grad_w3.reshape(8),
    )


def solution(mesh):
    placed = (
        P(("grp", "shard"), None),
        P(("grp", "shard"), None, None),
        P(("grp", "shard")),
        P(("grp", "shard"), None),
        P(("grp", "shard"), None, None),
        P(("grp", "shard"), None),
        P(),
        P(),
        P(),
        P(),
        P(),
        P(("grp", "shard"), None),
    )
    return jax.shard_map(
        shards,
        mesh=mesh,
        in_specs=placed,
        out_specs=(
            P("grp", "shard", None),
            P("grp", None),
            P("grp"),
            P("grp", None),
            P("grp"),
            P("grp"),
        ),
        check_vma=False,
    )
```

```python
import jax
import jax.numpy as jnp
from jax import lax
from jax.experimental import pallas as pl
from jax.experimental.pallas import tpu as pltpu
from jax.sharding import PartitionSpec as P

ROWS_DEV = 2048
E = 128
OWNERS = 48
HALF = 24
BLOCK = 32
NX = 4
PIECE = 6
SLOTS = 1024
VMEM_LIMIT = 24 * 1024 * 1024


def in_hbm(*values):
    return [pltpu.with_memory_space_constraint(v, pltpu.HBM) for v in values]


def iota(shape, dim):
    return lax.broadcasted_iota(jnp.int32, shape, dim)


def split(rows):
    high = rows.astype(jnp.bfloat16)
    low = (rows - high.astype(jnp.float32)).astype(jnp.bfloat16)
    return jnp.concatenate([high, low], axis=1)


CHUNK = 512
QUARTER = 24
SIDE = 2 * QUARTER
PART = NX * QUARTER


def sigmoid(z):
    return 0.5 * jnp.tanh(0.5 * z) + 0.5


def place(g, side):
    core, y0, y1, y2 = g & 1, (g >> 1) & 1, (g >> 2) & 1, (g >> 3) & 1
    return y0 * 16 + core * 8 + side * 4 + (y1 ^ y2) * 2 + y2


def dense_kernel(
    lengths_in, target_in, hist_in, pg_in, w1_in, b1_in, w2_in, b2_in, w3_in, ids_in, blocks_in,
    drow_ref, part_ref, ids_ref, blocks_ref,
    lengths_ref, target_ref, hist_ref, pg_ref, w1_ref, b1_ref, w2_ref, b2_ref, w3_ref,
    feats, act1s, dz2s, dz1s, sems,
):
    inputs = (hist_in, w1_in, target_in, b1_in, w2_in, b2_in, w3_in, pg_in, lengths_in, ids_in, blocks_in)
    held = (hist_ref, w1_ref, target_ref, b1_ref, w2_ref, b2_ref, w3_ref, pg_ref, lengths_ref, ids_ref, blocks_ref)
    copies = [pltpu.make_async_copy(a, b, sems.at[k]) for k, (a, b) in enumerate(zip(inputs, held))]
    for copy in copies:
        copy.start()
    for copy in copies:
        copy.wait()
    query = target_ref[...].astype(jnp.float32)
    w1, w2, w3 = w1_ref[...], w2_ref[...], w3_ref[...]
    grad_w3 = jnp.zeros((1, E), jnp.float32)
    grad_b2 = jnp.zeros((1, E), jnp.float32)
    grad_b1 = jnp.zeros((1, 2 * E), jnp.float32)
    samples = CHUNK // 128
    across = (((1,), (1,)), ((), ()))
    down = (((0,), (0,)), ((), ()))
    for c in range(SLOTS // CHUNK):
        rows = slice(c * CHUNK, (c + 1) * CHUNK)
        hist_low = hist_ref[rows, :]
        hist = hist_low.astype(jnp.float32)
        def spread(rows_of):
            parts = [rows_of[b : b + 1, :] for b in range(c * samples, (c + 1) * samples)]
            return jnp.concatenate([jnp.broadcast_to(v, (128, E)) for v in parts], axis=0)
        q = spread(query)
        pg = spread(pg_ref)
        live = jnp.concatenate(
            [iota((128, 1), 0) < lengths_ref[b] for b in range(c * samples, (c + 1) * samples)], axis=0
        )
        feat = jnp.concatenate(
            [q.astype(jnp.bfloat16), hist_low, (q - hist).astype(jnp.bfloat16), (q * hist).astype(jnp.bfloat16)],
            axis=1,
        )
        feats[rows, :] = feat
        act1 = sigmoid(jnp.dot(feat, w1, preferred_element_type=jnp.float32) + b1_ref[...])
        act1_low = act1.astype(jnp.bfloat16)
        act1s[rows, :] = act1_low
        act2 = sigmoid(jnp.dot(act1_low, w2, preferred_element_type=jnp.float32) + b2_ref[...])
        score = jnp.where(live, jnp.sum(act2 * w3, axis=1, keepdims=True), 0.0)
        dscore = jnp.where(live, jnp.sum(pg * hist, axis=1, keepdims=True), 0.0)
        dact2 = dscore * act2
        grad_w3 += jnp.sum(dact2, axis=0, keepdims=True)
        dz2_full = dact2 * w3 * (1.0 - act2)
        grad_b2 += jnp.sum(dz2_full, axis=0, keepdims=True)
        dz2 = dz2_full.astype(jnp.bfloat16)
        dz2s[rows, :] = dz2
        back = lax.dot_general(dz2, w2, across, preferred_element_type=jnp.float32)
        dz1_full = back * act1 * (1.0 - act1)
        grad_b1 += jnp.sum(dz1_full, axis=0, keepdims=True)
        dz1 = dz1_full.astype(jnp.bfloat16)
        dz1s[rows, :] = dz1
        dfeat = lax.dot_general(dz1, w1[E:, :], across, preferred_element_type=jnp.float32)
        drow_ref[rows, :] = dfeat[:, :E] - dfeat[:, E : 2 * E] + dfeat[:, 2 * E :] * q + score * pg

    grad_w1 = lax.dot_general(feats[...], dz1s[...], down, preferred_element_type=jnp.float32)
    grad_w2 = lax.dot_general(act1s[...], dz2s[...], down, preferred_element_type=jnp.float32)
    sub = iota((8, E), 0)
    small = jnp.where(sub == 0, grad_b1[:, :E], jnp.where(sub == 1, grad_b1[:, E:], 0.0))
    small = jnp.where(sub == 2, grad_b2, jnp.where(sub == 3, grad_w3, small))
    for g in range(16):
        for k in range(NX):
            base = place(g, k // 2) * SIDE + (k % 2) * QUARTER
            top = 32 * g + 16 * (k % 2)
            side = E * (k // 2)
            part_ref[base : base + 16, :] = grad_w1[top : top + 16, side : side + E]
            if k < 2:
                last = grad_w2[16 * g + 8 * k : 16 * g + 8 * k + 8, :]
            else:
                last = small
            part_ref[base + 16 : base + 24, :] = last


def dense(lengths, target, hist, pg, w1, b1, w2, b2, w3, ids, blocks):
    whole = pl.BlockSpec(memory_space=pltpu.VMEM)
    return pl.pallas_call(
        dense_kernel,
        out_shape=[
            jax.ShapeDtypeStruct((SLOTS, E), jnp.float32),
            jax.ShapeDtypeStruct((16 * PART, E), jnp.float32),
            jax.ShapeDtypeStruct(ids.shape, ids.dtype),
            jax.ShapeDtypeStruct(blocks.shape, blocks.dtype),
        ],
        in_specs=[pl.BlockSpec(memory_space=pltpu.HBM)] * 11,
        out_specs=[whole] * 4,
        scratch_shapes=[pltpu.SMEM(lengths.shape, lengths.dtype)]
        + [pltpu.VMEM(v.shape, v.dtype) for v in (target, hist, pg, w1, b1, w2, b2, w3)]
        + [
            pltpu.VMEM((SLOTS, 4 * E), jnp.bfloat16),
            pltpu.VMEM((SLOTS, 2 * E), jnp.bfloat16),
            pltpu.VMEM((SLOTS, E), jnp.bfloat16),
            pltpu.VMEM((SLOTS, 2 * E), jnp.bfloat16),
            pltpu.SemaphoreType.DMA((11,)),
        ],
        compiler_params=pltpu.CompilerParams(vmem_limit_bytes=VMEM_LIMIT),
        cost_estimate=pl.CostEstimate(
            flops=1_100_000_000, bytes_accessed=2_200_000, transcendentals=400_000
        ),
        name="dense",
    )(*in_hbm(lengths, target, hist, pg, w1, b1, w2, b2, w3, ids, blocks))


def pack_kernel(
    me_ref, counts_in, drow_ref, ids_ref, blocks_ref, send_ref, counts_ref, pick, source, sem
):
    fetch = pltpu.make_async_copy(counts_in, counts_ref, sem)
    fetch.start()
    me = me_ref[0]

    source[:, : 2 * E] = split(drow_ref[...])
    ids = ids_ref[...] & (ROWS_DEV - 1)
    id_columns = jnp.transpose(ids.astype(jnp.float32))
    for b in range(8):
        column = jnp.broadcast_to(id_columns[:, b : b + 1], (128, 128)).astype(jnp.int32)
        source[b * 128 : (b + 1) * 128, 2 * E : 3 * E] = (column >> 8).astype(jnp.float32).astype(jnp.bfloat16)
        source[b * 128 : (b + 1) * 128, 3 * E :] = (column & 255).astype(jnp.float32).astype(jnp.bfloat16)

    slot = iota((8, SLOTS), 1).astype(jnp.float32)[:1]
    eye = iota((HALF, OWNERS), 0) == iota((HALF, OWNERS), 1)
    def one_hot(mask, row):
        chosen = jnp.where(mask, row.astype(jnp.float32), 0.0)
        column = jnp.sum(chosen, axis=1, keepdims=True)
        return jnp.where(column == slot, 1.0, 0.0)
    for o in range(0, OWNERS, 2):
        pair = [one_hot(eye, blocks_ref[k : k + 1, :]) for k in (o, o + 1)]
        pick[o * HALF : (o + 2) * HALF, :] = jnp.concatenate(pair, axis=0).astype(jnp.bfloat16)
    fetch.wait()
    hot = jnp.int32(0)
    for o in range(OWNERS):
        hot = jnp.where(counts_ref[0, o] > HALF, jnp.int32(o), hot)
    r, lane = iota((32, OWNERS), 0), iota((32, OWNERS), 1)
    late = (lane == HALF + PIECE * (r // 8) + r % 8) & (r % 8 < PIECE)
    last = one_hot(late, blocks_ref[pl.ds(hot, 1), :])
    pick[OWNERS * HALF :, :] = last.astype(jnp.bfloat16)

    got = jnp.dot(pick[...], source[...], preferred_element_type=jnp.float32)

    sub, lane = iota((HALF, E), 0), iota((HALF, E), 1)
    place = lane - sub == (me % NX) * BLOCK
    sub8, lane8 = iota((8, E), 0), iota((8, E), 1)
    place8 = (lane8 - sub8 == (me % 16) * 8) & (sub8 < PIECE)
    tails = []
    for x in range(NX):
        part = got[OWNERS * HALF + 8 * x : OWNERS * HALF + 8 * x + 8]
        where_to = part[:, 2 * E : 3 * E] * 256.0 + part[:, 3 * E :] + 1.0
        row = jnp.sum(jnp.where(place8, where_to, 0.0), axis=0, keepdims=True)
        tails.append(jnp.where(sub8 < PIECE, part[:, :E] + part[:, E : 2 * E], row))
    for o in range(OWNERS):
        part = got[o * HALF : (o + 1) * HALF]
        send_ref[o, :HALF, :] = part[:, :E] + part[:, E : 2 * E]
        where_to = part[:, 2 * E : 3 * E] * 256.0 + part[:, 3 * E :] + 1.0
        used = place & (sub < counts_ref[0, o])
        row = jnp.sum(jnp.where(used, where_to, 0.0), axis=0, keepdims=True)
        send_ref[o, HALF:, :] = jnp.where(sub8 == PIECE, row, tails[o % NX])


def pack(me, counts, drow, ids, blocks):
    whole = pl.BlockSpec(memory_space=pltpu.VMEM)
    scalar = pl.BlockSpec(memory_space=pltpu.SMEM)
    return pl.pallas_call(
        pack_kernel,
        out_shape=jax.ShapeDtypeStruct((OWNERS, BLOCK, E), jnp.float32),
        in_specs=[scalar, pl.BlockSpec(memory_space=pltpu.HBM), whole, whole, whole],
        out_specs=whole,
        scratch_shapes=[
            pltpu.SMEM(counts.shape, counts.dtype),
            pltpu.VMEM((OWNERS * HALF + 32, SLOTS), jnp.bfloat16),
            pltpu.VMEM((SLOTS, 4 * E), jnp.bfloat16),
            pltpu.SemaphoreType.DMA(()),
        ],
        compiler_params=pltpu.CompilerParams(vmem_limit_bytes=VMEM_LIMIT),
        cost_estimate=pl.CostEstimate(
            flops=2 * 1184 * 1024 * 512, bytes_accessed=2_000_000, transcendentals=0
        ),
        name="pack",
    )(me, *in_hbm(counts), drow, ids, blocks)


STEP = 512


def product(t, dest, rows):
    table_row = (iota((STEP, E), 0) + (t * STEP + 1)).astype(jnp.float32)
    hits = [
        jnp.where(table_row == dest[0:1, k : k + 128], 1.0, 0.0).astype(jnp.bfloat16)
        for k in range(0, OWNERS * BLOCK, 128)
    ]
    both = jnp.dot(jnp.concatenate(hits, axis=1), rows[...], preferred_element_type=jnp.float32)
    return both[:, :E] + both[:, E:]


SCATTER_SCRATCH = [
    pltpu.VMEM((OWNERS * BLOCK, 2 * E), jnp.bfloat16),
    pltpu.VMEM((8, OWNERS * BLOCK), jnp.float32),
]
SCATTER_COST = pl.CostEstimate(flops=2 * 2048 * 1536 * 256, bytes_accessed=2_500_000, transcendentals=0)


def add_main_kernel(got_ref, table_ref, rows, dest):
    for g in range(OWNERS // NX):
        rows[g * 128 : (g + 1) * 128, :] = split(got_ref[g * 128 : (g + 1) * 128, :])
        total = sum(got_ref[(NX * g + j) * BLOCK + HALF : (NX * g + j + 1) * BLOCK, :] for j in range(NX))
        dest[:, g * 128 : (g + 1) * 128] = jnp.broadcast_to(total[PIECE : PIECE + 1, :], (8, E))
    for t in range(ROWS_DEV // STEP):
        table_ref[t * STEP : (t + 1) * STEP, :] = product(t, dest, rows)


def add_main(got):
    whole = pl.BlockSpec(memory_space=pltpu.VMEM)
    return pl.pallas_call(
        add_main_kernel,
        out_shape=jax.ShapeDtypeStruct((ROWS_DEV, E), jnp.float32),
        in_specs=[whole],
        out_specs=whole,
        scratch_shapes=SCATTER_SCRATCH,
        compiler_params=pltpu.CompilerParams(vmem_limit_bytes=VMEM_LIMIT),
        cost_estimate=SCATTER_COST,
        name="add_main",
    )(got)


def add_late_kernel(
    me_ref, counts_ref, table_in, own_in, late0_in, late1_in, late2_in, table_out,
    table, late, rows, dest, sems,
):
    @pl.when(counts_ref[0, me_ref[0]] > HALF)
    def _():
        slabs = (own_in, late0_in, late1_in, late2_in)
        fetches = [pltpu.make_async_copy(slabs[k], late.at[k], sems.at[k]) for k in range(NX)]
        fetches.append(pltpu.make_async_copy(table_in, table, sems.at[NX]))
        for fetch in fetches:
            fetch.start()
        for fetch in fetches:
            fetch.wait()
        for k in range(NX):
            for g in range(3):
                tiles = [late[k, s * 8 : s * 8 + 8, :] for s in range(16 * g, 16 * g + 16)]
                at = (k * 3 + g) * 128
                rows[at : at + 128, :] = split(jnp.concatenate(tiles, axis=0))
                dest[:, at : at + 128] = jnp.broadcast_to(sum(tiles)[7:8, :], (8, E))
        for t in range(ROWS_DEV // STEP):
            table[t * STEP : (t + 1) * STEP, :] += product(t, dest, rows)
        write = pltpu.make_async_copy(table, table_out, sems.at[NX])
        write.start()
        write.wait()


def add_late(me, counts, table, late):
    scalar = pl.BlockSpec(memory_space=pltpu.SMEM)
    anywhere = pl.BlockSpec(memory_space=pl.ANY)
    return pl.pallas_call(
        add_late_kernel,
        out_shape=jax.ShapeDtypeStruct((ROWS_DEV, E), jnp.float32),
        in_specs=[scalar, scalar] + [anywhere] * 5,
        out_specs=anywhere,
        scratch_shapes=[
            pltpu.VMEM((ROWS_DEV, E), jnp.float32),
            pltpu.VMEM((NX, OWNERS * 8, E), jnp.float32),
        ]
        + SCATTER_SCRATCH
        + [pltpu.SemaphoreType.DMA((NX + 1,))],
        input_output_aliases={2: 0},
        compiler_params=pltpu.CompilerParams(vmem_limit_bytes=VMEM_LIMIT),
        cost_estimate=SCATTER_COST,
        name="add_late",
    )(me, counts, table, *late)


STEPS = (("grp", 2), ("grp", 1), ("shard", 1), ("grp", 4), ("grp", 12))
NZ = OWNERS // NX
Z_GROUPS = [[z * NX + x for z in range(NZ)] for x in range(NX)]


def swap(value, axis, bits):
    size = lax.axis_size(axis)
    return lax.ppermute(value, axis, [(i, i ^ bits) for i in range(size)])


def join_kernel(keep_ref, there_ref, got_ref, copies_ref, slab_ref):
    part = keep_ref[...] + there_ref[...]
    for z in range(NZ):
        copies_ref[z] = part
    for s in range(OWNERS):
        slab_ref[s * 8 : s * 8 + 8, :] = got_ref[s * BLOCK + HALF : (s + 1) * BLOCK, :]


def join(keep, there, got):
    whole = pl.BlockSpec(memory_space=pltpu.VMEM)
    return pl.pallas_call(
        join_kernel,
        out_shape=[
            jax.ShapeDtypeStruct((NZ, SIDE, E), jnp.float32),
            jax.ShapeDtypeStruct((OWNERS * 8, E), jnp.float32),
        ],
        in_specs=[whole, whole, whole],
        out_specs=[whole, whole],
        compiler_params=pltpu.CompilerParams(vmem_limit_bytes=VMEM_LIMIT),
        cost_estimate=pl.CostEstimate(flops=3072, bytes_accessed=1_300_000, transcendentals=0),
        name="join",
    )(keep, there, got)


def add_kernel_z(parts_ref, out_ref):
    part = parts_ref[0]
    for z in range(1, NZ):
        part += parts_ref[z]
    out_ref[...] = part


def add_parts(parts):
    whole = pl.BlockSpec(memory_space=pltpu.VMEM)
    return pl.pallas_call(
        add_kernel_z,
        out_shape=jax.ShapeDtypeStruct((SIDE, E), jnp.float32),
        in_specs=[whole],
        out_specs=whole,
        compiler_params=pltpu.CompilerParams(vmem_limit_bytes=VMEM_LIMIT),
        cost_estimate=pl.CostEstimate(flops=67584, bytes_accessed=320_000, transcendentals=0),
        name="add_parts",
    )(parts)


def final_kernel(g_ref, side_ref, mine_ref, other_ref, w1_ref, b1_ref, w2_ref, b2_ref, w3_ref):
    g, first = g_ref[0], side_ref[0] == 0
    mine, other = mine_ref[...], other_ref[...]
    low, high = jnp.where(first, mine, other), jnp.where(first, other, mine)
    quarters = [low[:QUARTER], low[QUARTER:], high[:QUARTER], high[QUARTER:]]
    for k in range(NX):
        top, side = 16 * (k % 2), E * (k // 2)
        w1_ref[top : top + 16, side : side + E] = quarters[k][:16]
    w2_ref[:8, :] = quarters[0][16:]
    w2_ref[8:, :] = quarters[1][16:]
    small = quarters[2][16:]
    by16 = pltpu.roll(small, (128 - (g % 8) * 16) % 128, 1)
    by8 = pltpu.roll(small, (128 - g * 8) % 128, 1)
    b1_ref[...] = jnp.where(g < 8, by16[0:1, :16], by16[1:2, :16])
    b2_ref[...] = by8[2:3, :8]
    w3_ref[...] = by8[3:4, :8]


def final(g, side, mine, other):
    whole = pl.BlockSpec(memory_space=pltpu.VMEM)
    shapes = ((32, 2 * E), (1, 16), (16, E), (1, 8), (1, 8))
    return pl.pallas_call(
        final_kernel,
        out_shape=[jax.ShapeDtypeStruct(shape, jnp.float32) for shape in shapes],
        in_specs=[pl.BlockSpec(memory_space=pltpu.SMEM)] * 2 + [whole, whole],
        out_specs=[whole] * 5,
        compiler_params=pltpu.CompilerParams(vmem_limit_bytes=VMEM_LIMIT),
        cost_estimate=pl.CostEstimate(flops=1024, bytes_accessed=100_000, transcendentals=0),
        name="final",
    )(g, side, mine, other)


def shards(
    target,
    history,
    lengths,
    hist_ids,
    block_rows,
    block_counts,
    attn_w1,
    attn_b1,
    attn_w2,
    attn_b2,
    attn_w3,
    pooled_gradient,
):
    g = lax.axis_index("grp")
    me = lax.axis_index("shard").reshape(1)
    drow, part, ids, blocks = dense(
        lengths,
        target,
        history.reshape(SLOTS, E),
        pooled_gradient,
        attn_w1,
        attn_b1.reshape(1, 2 * E),
        attn_w2,
        attn_b2.reshape(1, E),
        attn_w3.reshape(1, E),
        hist_ids,
        block_rows[0],
    )
    send = pack(me, block_counts, drow, ids, blocks)
    got = lax.all_to_all(send, "shard", split_axis=0, concat_axis=0, tiled=True)
    got = got.reshape(OWNERS * BLOCK, E)

    part = part.reshape(2, 2, 2, 2, 2, SIDE, E)
    y2 = (g >> 3) & 1
    side = (me[0] ^ (me[0] >> 1)) & 1
    bits = ((g >> 1) & 1, g & 1, side, ((g >> 2) & 1) ^ y2, y2)
    for bit, (axis, k) in zip(bits, STEPS):
        keep = lax.dynamic_index_in_dim(part, bit, 0, False)
        away = lax.dynamic_index_in_dim(part, 1 - bit, 0, False)
        part = keep + swap(away, axis, k)
    copies, slab = join(part, swap(part, "shard", 3), got)
    parts = lax.all_to_all(
        copies, "shard", split_axis=0, concat_axis=0, tiled=True, axis_index_groups=Z_GROUPS
    )
    total = add_parts(parts)
    other = swap(total, "shard", 1)
    late = [slab]
    for turn in (1, 2, 3):
        pairs = [(s, s // NX * NX + (s + turn) % NX) for s in range(OWNERS)]
        late.append(lax.ppermute(slab, "shard", pairs))
    table = add_late(me, block_counts, add_main(got), late)
    grad_w1, grad_b1, grad_w2, grad_b2, grad_w3 = final(g.reshape(1), side.reshape(1), total, other)
    return (
        table[None],
        grad_w1,
        grad_b1.reshape(16),
        grad_w2,
        grad_b2.reshape(8),
        grad_w3.reshape(8),
    )


def solution(mesh):
    placed = (
        P(("grp", "shard"), None),
        P(("grp", "shard"), None, None),
        P(("grp", "shard")),
        P(("grp", "shard"), None),
        P(("grp", "shard"), None, None),
        P(("grp", "shard"), None),
        P(),
        P(),
        P(),
        P(),
        P(),
        P(("grp", "shard"), None),
    )
    return jax.shard_map(
        shards,
        mesh=mesh,
        in_specs=placed,
        out_specs=(
            P("grp", "shard", None),
            P("grp", None),
            P("grp"),
            P("grp", None),
            P("grp"),
            P("grp"),
        ),
        check_vma=False,
    )
```

```python
import jax
import jax.numpy as jnp
from jax import lax
from jax.experimental import pallas as pl
from jax.experimental.pallas import tpu as pltpu
from jax.sharding import PartitionSpec as P

ROWS_DEV = 2048
E = 128
OWNERS = 48
HALF = 24
BLOCK = 32
NX = 4
PIECE = 6
SLOTS = 1024
VMEM_LIMIT = 24 * 1024 * 1024


def in_hbm(*values):
    return [pltpu.with_memory_space_constraint(v, pltpu.HBM) for v in values]


def iota(shape, dim):
    return lax.broadcasted_iota(jnp.int32, shape, dim)


def split(rows):
    high = rows.astype(jnp.bfloat16)
    low = (rows - high.astype(jnp.float32)).astype(jnp.bfloat16)
    return jnp.concatenate([high, low], axis=1)


CHUNK = 512
QUARTER = 24
SIDE = 2 * QUARTER
PART = NX * QUARTER


def sigmoid(z):
    return 0.5 * jnp.tanh(0.5 * z) + 0.5


def place(g, side):
    core, y0, y1, y2 = g & 1, (g >> 1) & 1, (g >> 2) & 1, (g >> 3) & 1
    return y0 * 16 + core * 8 + side * 4 + (y1 ^ y2) * 2 + y2


def dense_kernel(
    target_ref, lengths_in, hist_in, pg_in, w1_in, b1_in, w2_in, b2_in, w3_in, ids_in, blocks_in,
    drow_ref, part_ref, ids_ref, blocks_ref,
    lengths_ref, hist_ref, pg_ref, w1_ref, b1_ref, w2_ref, b2_ref, w3_ref,
    feats, act1s, dz2s, dz1s, sems,
):
    inputs = (hist_in, w1_in, b1_in, w2_in, b2_in, w3_in, pg_in, lengths_in, ids_in, blocks_in)
    held = (hist_ref, w1_ref, b1_ref, w2_ref, b2_ref, w3_ref, pg_ref, lengths_ref, ids_ref, blocks_ref)
    copies = [pltpu.make_async_copy(a, b, sems.at[k]) for k, (a, b) in enumerate(zip(inputs, held))]
    for copy in copies:
        copy.start()
    for copy in copies:
        copy.wait()
    query = target_ref[...]
    w1, w2, w3 = w1_ref[...], w2_ref[...], w3_ref[...]
    grad_w3 = jnp.zeros((1, E), jnp.float32)
    grad_b2 = jnp.zeros((1, E), jnp.float32)
    grad_b1 = jnp.zeros((1, 2 * E), jnp.float32)
    samples = CHUNK // 128
    across = (((1,), (1,)), ((), ()))
    down = (((0,), (0,)), ((), ()))
    for c in range(SLOTS // CHUNK):
        rows = slice(c * CHUNK, (c + 1) * CHUNK)
        hist_low = hist_ref[rows, :]
        hist = hist_low.astype(jnp.float32)
        def spread(rows_of):
            parts = [rows_of[b : b + 1, :] for b in range(c * samples, (c + 1) * samples)]
            return jnp.concatenate([jnp.broadcast_to(v, (128, E)) for v in parts], axis=0)
        q = spread(query)
        pg = spread(pg_ref)
        live = jnp.concatenate(
            [iota((128, 1), 0) < lengths_ref[b] for b in range(c * samples, (c + 1) * samples)], axis=0
        )
        feat = jnp.concatenate(
            [q.astype(jnp.bfloat16), hist_low, (q - hist).astype(jnp.bfloat16), (q * hist).astype(jnp.bfloat16)],
            axis=1,
        )
        feats[rows, :] = feat
        act1 = sigmoid(jnp.dot(feat, w1, preferred_element_type=jnp.float32) + b1_ref[...])
        act1_low = act1.astype(jnp.bfloat16)
        act1s[rows, :] = act1_low
        act2 = sigmoid(jnp.dot(act1_low, w2, preferred_element_type=jnp.float32) + b2_ref[...])
        score = jnp.where(live, jnp.sum(act2 * w3, axis=1, keepdims=True), 0.0)
        dscore = jnp.where(live, jnp.sum(pg * hist, axis=1, keepdims=True), 0.0)
        dact2 = dscore * act2
        grad_w3 += jnp.sum(dact2, axis=0, keepdims=True)
        dz2_full = dact2 * w3 * (1.0 - act2)
        grad_b2 += jnp.sum(dz2_full, axis=0, keepdims=True)
        dz2 = dz2_full.astype(jnp.bfloat16)
        dz2s[rows, :] = dz2
        back = lax.dot_general(dz2, w2, across, preferred_element_type=jnp.float32)
        dz1_full = back * act1 * (1.0 - act1)
        grad_b1 += jnp.sum(dz1_full, axis=0, keepdims=True)
        dz1 = dz1_full.astype(jnp.bfloat16)
        dz1s[rows, :] = dz1
        dfeat = lax.dot_general(dz1, w1[E:, :], across, preferred_element_type=jnp.float32)
        drow_ref[rows, :] = dfeat[:, :E] - dfeat[:, E : 2 * E] + dfeat[:, 2 * E :] * q + score * pg

    grad_w1 = lax.dot_general(feats[...], dz1s[...], down, preferred_element_type=jnp.float32)
    grad_w2 = lax.dot_general(act1s[...], dz2s[...], down, preferred_element_type=jnp.float32)
    sub = iota((8, E), 0)
    small = jnp.where(sub == 0, grad_b1[:, :E], jnp.where(sub == 1, grad_b1[:, E:], 0.0))
    small = jnp.where(sub == 2, grad_b2, jnp.where(sub == 3, grad_w3, small))
    for g in range(16):
        for k in range(NX):
            base = place(g, k // 2) * SIDE + (k % 2) * QUARTER
            top = 32 * g + 16 * (k % 2)
            side = E * (k // 2)
            part_ref[base : base + 16, :] = grad_w1[top : top + 16, side : side + E]
            if k < 2:
                last = grad_w2[16 * g + 8 * k : 16 * g + 8 * k + 8, :]
            else:
                last = small
            part_ref[base + 16 : base + 24, :] = last


def dense(lengths, target, hist, pg, w1, b1, w2, b2, w3, ids, blocks):
    whole = pl.BlockSpec(memory_space=pltpu.VMEM)
    return pl.pallas_call(
        dense_kernel,
        out_shape=[
            jax.ShapeDtypeStruct((SLOTS, E), jnp.float32),
            jax.ShapeDtypeStruct((16 * PART, E), jnp.float32),
            jax.ShapeDtypeStruct(ids.shape, ids.dtype),
            jax.ShapeDtypeStruct(blocks.shape, blocks.dtype),
        ],
        in_specs=[whole] + [pl.BlockSpec(memory_space=pltpu.HBM)] * 10,
        out_specs=[whole] * 4,
        scratch_shapes=[pltpu.SMEM(lengths.shape, lengths.dtype)]
        + [pltpu.VMEM(v.shape, v.dtype) for v in (hist, pg, w1, b1, w2, b2, w3)]
        + [
            pltpu.VMEM((SLOTS, 4 * E), jnp.bfloat16),
            pltpu.VMEM((SLOTS, 2 * E), jnp.bfloat16),
            pltpu.VMEM((SLOTS, E), jnp.bfloat16),
            pltpu.VMEM((SLOTS, 2 * E), jnp.bfloat16),
            pltpu.SemaphoreType.DMA((10,)),
        ],
        compiler_params=pltpu.CompilerParams(vmem_limit_bytes=VMEM_LIMIT),
        cost_estimate=pl.CostEstimate(
            flops=1_100_000_000, bytes_accessed=2_200_000, transcendentals=400_000
        ),
        name="dense",
    )(target, *in_hbm(lengths, hist, pg, w1, b1, w2, b2, w3, ids, blocks))


def pack_kernel(
    me_ref, counts_in, drow_ref, ids_ref, blocks_ref, send_ref, counts_ref, pick, source, sem
):
    fetch = pltpu.make_async_copy(counts_in, counts_ref, sem)
    fetch.start()
    me = me_ref[0]

    source[:, : 2 * E] = split(drow_ref[...])
    ids = ids_ref[...] & (ROWS_DEV - 1)
    id_columns = jnp.transpose(ids.astype(jnp.float32))
    for b in range(8):
        column = jnp.broadcast_to(id_columns[:, b : b + 1], (128, 128)).astype(jnp.int32)
        source[b * 128 : (b + 1) * 128, 2 * E : 3 * E] = (column >> 8).astype(jnp.float32).astype(jnp.bfloat16)
        source[b * 128 : (b + 1) * 128, 3 * E :] = (column & 255).astype(jnp.float32).astype(jnp.bfloat16)

    slot = iota((8, SLOTS), 1).astype(jnp.float32)[:1]
    eye = iota((HALF, OWNERS), 0) == iota((HALF, OWNERS), 1)
    def one_hot(mask, row):
        chosen = jnp.where(mask, row.astype(jnp.float32), 0.0)
        column = jnp.sum(chosen, axis=1, keepdims=True)
        return jnp.where(column == slot, 1.0, 0.0)
    for o in range(0, OWNERS, 2):
        pair = [one_hot(eye, blocks_ref[k : k + 1, :]) for k in (o, o + 1)]
        pick[o * HALF : (o + 2) * HALF, :] = jnp.concatenate(pair, axis=0).astype(jnp.bfloat16)
    fetch.wait()
    hot = jnp.int32(0)
    for o in range(OWNERS):
        hot = jnp.where(counts_ref[0, o] > HALF, jnp.int32(o), hot)
    r, lane = iota((32, OWNERS), 0), iota((32, OWNERS), 1)
    late = (lane == HALF + PIECE * (r // 8) + r % 8) & (r % 8 < PIECE)
    last = one_hot(late, blocks_ref[pl.ds(hot, 1), :])
    pick[OWNERS * HALF :, :] = last.astype(jnp.bfloat16)

    got = jnp.dot(pick[...], source[...], preferred_element_type=jnp.float32)

    sub, lane = iota((HALF, E), 0), iota((HALF, E), 1)
    place = lane - sub == (me % NX) * BLOCK
    sub8, lane8 = iota((8, E), 0), iota((8, E), 1)
    place8 = (lane8 - sub8 == (me % 16) * 8) & (sub8 < PIECE)
    tails = []
    for x in range(NX):
        part = got[OWNERS * HALF + 8 * x : OWNERS * HALF + 8 * x + 8]
        where_to = part[:, 2 * E : 3 * E] * 256.0 + part[:, 3 * E :] + 1.0
        row = jnp.sum(jnp.where(place8, where_to, 0.0), axis=0, keepdims=True)
        tails.append(jnp.where(sub8 < PIECE, part[:, :E] + part[:, E : 2 * E], row))
    for o in range(OWNERS):
        part = got[o * HALF : (o + 1) * HALF]
        send_ref[o, :HALF, :] = part[:, :E] + part[:, E : 2 * E]
        where_to = part[:, 2 * E : 3 * E] * 256.0 + part[:, 3 * E :] + 1.0
        used = place & (sub < counts_ref[0, o])
        row = jnp.sum(jnp.where(used, where_to, 0.0), axis=0, keepdims=True)
        send_ref[o, HALF:, :] = jnp.where(sub8 == PIECE, row, tails[o % NX])


def pack(me, counts, drow, ids, blocks):
    whole = pl.BlockSpec(memory_space=pltpu.VMEM)
    scalar = pl.BlockSpec(memory_space=pltpu.SMEM)
    return pl.pallas_call(
        pack_kernel,
        out_shape=jax.ShapeDtypeStruct((OWNERS, BLOCK, E), jnp.float32),
        in_specs=[scalar, pl.BlockSpec(memory_space=pltpu.HBM), whole, whole, whole],
        out_specs=whole,
        scratch_shapes=[
            pltpu.SMEM(counts.shape, counts.dtype),
            pltpu.VMEM((OWNERS * HALF + 32, SLOTS), jnp.bfloat16),
            pltpu.VMEM((SLOTS, 4 * E), jnp.bfloat16),
            pltpu.SemaphoreType.DMA(()),
        ],
        compiler_params=pltpu.CompilerParams(vmem_limit_bytes=VMEM_LIMIT),
        cost_estimate=pl.CostEstimate(
            flops=2 * 1184 * 1024 * 512, bytes_accessed=2_000_000, transcendentals=0
        ),
        name="pack",
    )(me, *in_hbm(counts), drow, ids, blocks)


STEP = 512


def product(t, dest, rows):
    table_row = (iota((STEP, E), 0) + (t * STEP + 1)).astype(jnp.float32)
    hits = [
        jnp.where(table_row == dest[0:1, k : k + 128], 1.0, 0.0).astype(jnp.bfloat16)
        for k in range(0, OWNERS * BLOCK, 128)
    ]
    both = jnp.dot(jnp.concatenate(hits, axis=1), rows[...], preferred_element_type=jnp.float32)
    return both[:, :E] + both[:, E:]


SCATTER_SCRATCH = [
    pltpu.VMEM((OWNERS * BLOCK, 2 * E), jnp.bfloat16),
    pltpu.VMEM((8, OWNERS * BLOCK), jnp.float32),
]
SCATTER_COST = pl.CostEstimate(flops=2 * 2048 * 1536 * 256, bytes_accessed=2_500_000, transcendentals=0)


def add_main_kernel(got_ref, table_ref, rows, dest):
    for g in range(OWNERS // NX):
        rows[g * 128 : (g + 1) * 128, :] = split(got_ref[g * 128 : (g + 1) * 128, :])
        total = sum(got_ref[(NX * g + j) * BLOCK + HALF : (NX * g + j + 1) * BLOCK, :] for j in range(NX))
        dest[:, g * 128 : (g + 1) * 128] = jnp.broadcast_to(total[PIECE : PIECE + 1, :], (8, E))
    for t in range(ROWS_DEV // STEP):
        table_ref[t * STEP : (t + 1) * STEP, :] = product(t, dest, rows)


def add_main(got):
    whole = pl.BlockSpec(memory_space=pltpu.VMEM)
    return pl.pallas_call(
        add_main_kernel,
        out_shape=jax.ShapeDtypeStruct((ROWS_DEV, E), jnp.float32),
        in_specs=[whole],
        out_specs=whole,
        scratch_shapes=SCATTER_SCRATCH,
        compiler_params=pltpu.CompilerParams(vmem_limit_bytes=VMEM_LIMIT),
        cost_estimate=SCATTER_COST,
        name="add_main",
    )(got)


def add_late_kernel(
    me_ref, counts_ref, table_in, own_in, late0_in, late1_in, late2_in, table_out,
    table, late, rows, dest, sems,
):
    @pl.when(counts_ref[0, me_ref[0]] > HALF)
    def _():
        slabs = (own_in, late0_in, late1_in, late2_in)
        fetches = [pltpu.make_async_copy(slabs[k], late.at[k], sems.at[k]) for k in range(NX)]
        fetches.append(pltpu.make_async_copy(table_in, table, sems.at[NX]))
        for fetch in fetches:
            fetch.start()
        for fetch in fetches:
            fetch.wait()
        for k in range(NX):
            for g in range(3):
                tiles = [late[k, s * 8 : s * 8 + 8, :] for s in range(16 * g, 16 * g + 16)]
                at = (k * 3 + g) * 128
                rows[at : at + 128, :] = split(jnp.concatenate(tiles, axis=0))
                dest[:, at : at + 128] = jnp.broadcast_to(sum(tiles)[7:8, :], (8, E))
        for t in range(ROWS_DEV // STEP):
            table[t * STEP : (t + 1) * STEP, :] += product(t, dest, rows)
        write = pltpu.make_async_copy(table, table_out, sems.at[NX])
        write.start()
        write.wait()


def add_late(me, counts, table, late):
    scalar = pl.BlockSpec(memory_space=pltpu.SMEM)
    anywhere = pl.BlockSpec(memory_space=pl.ANY)
    return pl.pallas_call(
        add_late_kernel,
        out_shape=jax.ShapeDtypeStruct((ROWS_DEV, E), jnp.float32),
        in_specs=[scalar, scalar] + [anywhere] * 5,
        out_specs=anywhere,
        scratch_shapes=[
            pltpu.VMEM((ROWS_DEV, E), jnp.float32),
            pltpu.VMEM((NX, OWNERS * 8, E), jnp.float32),
        ]
        + SCATTER_SCRATCH
        + [pltpu.SemaphoreType.DMA((NX + 1,))],
        input_output_aliases={2: 0},
        compiler_params=pltpu.CompilerParams(vmem_limit_bytes=VMEM_LIMIT),
        cost_estimate=SCATTER_COST,
        name="add_late",
    )(me, counts, table, *late)


STEPS = (("grp", 2), ("grp", 1), ("shard", 1), ("grp", 4), ("grp", 12))
NZ = OWNERS // NX
Z_GROUPS = [[z * NX + x for z in range(NZ)] for x in range(NX)]


def swap(value, axis, bits):
    size = lax.axis_size(axis)
    return lax.ppermute(value, axis, [(i, i ^ bits) for i in range(size)])


def join_kernel(keep_ref, there_ref, got_ref, copies_ref, slab_ref):
    part = keep_ref[...] + there_ref[...]
    for z in range(NZ):
        copies_ref[z] = part
    for s in range(OWNERS):
        slab_ref[s * 8 : s * 8 + 8, :] = got_ref[s * BLOCK + HALF : (s + 1) * BLOCK, :]


def join(keep, there, got):
    whole = pl.BlockSpec(memory_space=pltpu.VMEM)
    return pl.pallas_call(
        join_kernel,
        out_shape=[
            jax.ShapeDtypeStruct((NZ, SIDE, E), jnp.float32),
            jax.ShapeDtypeStruct((OWNERS * 8, E), jnp.float32),
        ],
        in_specs=[whole, whole, whole],
        out_specs=[whole, whole],
        compiler_params=pltpu.CompilerParams(vmem_limit_bytes=VMEM_LIMIT),
        cost_estimate=pl.CostEstimate(flops=3072, bytes_accessed=1_300_000, transcendentals=0),
        name="join",
    )(keep, there, got)


def add_kernel_z(parts_ref, out_ref):
    part = parts_ref[0]
    for z in range(1, NZ):
        part += parts_ref[z]
    out_ref[...] = part


def add_parts(parts):
    whole = pl.BlockSpec(memory_space=pltpu.VMEM)
    return pl.pallas_call(
        add_kernel_z,
        out_shape=jax.ShapeDtypeStruct((SIDE, E), jnp.float32),
        in_specs=[whole],
        out_specs=whole,
        compiler_params=pltpu.CompilerParams(vmem_limit_bytes=VMEM_LIMIT),
        cost_estimate=pl.CostEstimate(flops=67584, bytes_accessed=320_000, transcendentals=0),
        name="add_parts",
    )(parts)


def final_kernel(g_ref, side_ref, mine_ref, other_ref, w1_ref, b1_ref, w2_ref, b2_ref, w3_ref):
    g, first = g_ref[0], side_ref[0] == 0
    mine, other = mine_ref[...], other_ref[...]
    low, high = jnp.where(first, mine, other), jnp.where(first, other, mine)
    quarters = [low[:QUARTER], low[QUARTER:], high[:QUARTER], high[QUARTER:]]
    for k in range(NX):
        top, side = 16 * (k % 2), E * (k // 2)
        w1_ref[top : top + 16, side : side + E] = quarters[k][:16]
    w2_ref[:8, :] = quarters[0][16:]
    w2_ref[8:, :] = quarters[1][16:]
    small = quarters[2][16:]
    by16 = pltpu.roll(small, (128 - (g % 8) * 16) % 128, 1)
    by8 = pltpu.roll(small, (128 - g * 8) % 128, 1)
    b1_ref[...] = jnp.where(g < 8, by16[0:1, :16], by16[1:2, :16])
    b2_ref[...] = by8[2:3, :8]
    w3_ref[...] = by8[3:4, :8]


def final(g, side, mine, other):
    whole = pl.BlockSpec(memory_space=pltpu.VMEM)
    shapes = ((32, 2 * E), (1, 16), (16, E), (1, 8), (1, 8))
    return pl.pallas_call(
        final_kernel,
        out_shape=[jax.ShapeDtypeStruct(shape, jnp.float32) for shape in shapes],
        in_specs=[pl.BlockSpec(memory_space=pltpu.SMEM)] * 2 + [whole, whole],
        out_specs=[whole] * 5,
        compiler_params=pltpu.CompilerParams(vmem_limit_bytes=VMEM_LIMIT),
        cost_estimate=pl.CostEstimate(flops=1024, bytes_accessed=100_000, transcendentals=0),
        name="final",
    )(g, side, mine, other)


def shards(
    target,
    history,
    lengths,
    hist_ids,
    block_rows,
    block_counts,
    attn_w1,
    attn_b1,
    attn_w2,
    attn_b2,
    attn_w3,
    pooled_gradient,
):
    g = lax.axis_index("grp")
    me = lax.axis_index("shard").reshape(1)
    drow, part, ids, blocks = dense(
        lengths,
        target.astype(jnp.float32),
        history.reshape(SLOTS, E),
        pooled_gradient,
        attn_w1,
        attn_b1.reshape(1, 2 * E),
        attn_w2,
        attn_b2.reshape(1, E),
        attn_w3.reshape(1, E),
        hist_ids,
        block_rows[0],
    )
    send = pack(me, block_counts, drow, ids, blocks)
    got = lax.all_to_all(send, "shard", split_axis=0, concat_axis=0, tiled=True)
    got = got.reshape(OWNERS * BLOCK, E)

    part = part.reshape(2, 2, 2, 2, 2, SIDE, E)
    y2 = (g >> 3) & 1
    side = (me[0] ^ (me[0] >> 1)) & 1
    bits = ((g >> 1) & 1, g & 1, side, ((g >> 2) & 1) ^ y2, y2)
    for bit, (axis, k) in zip(bits, STEPS):
        keep = lax.dynamic_index_in_dim(part, bit, 0, False)
        away = lax.dynamic_index_in_dim(part, 1 - bit, 0, False)
        part = keep + swap(away, axis, k)
    copies, slab = join(part, swap(part, "shard", 3), got)
    parts = lax.all_to_all(
        copies, "shard", split_axis=0, concat_axis=0, tiled=True, axis_index_groups=Z_GROUPS
    )
    total = add_parts(parts)
    other = swap(total, "shard", 1)
    late = [slab]
    for turn in (1, 2, 3):
        pairs = [(s, s // NX * NX + (s + turn) % NX) for s in range(OWNERS)]
        late.append(lax.ppermute(slab, "shard", pairs))
    table = add_late(me, block_counts, add_main(got), late)
    grad_w1, grad_b1, grad_w2, grad_b2, grad_w3 = final(g.reshape(1), side.reshape(1), total, other)
    return (
        table[None],
        grad_w1,
        grad_b1.reshape(16),
        grad_w2,
        grad_b2.reshape(8),
        grad_w3.reshape(8),
    )


def solution(mesh):
    placed = (
        P(("grp", "shard"), None),
        P(("grp", "shard"), None, None),
        P(("grp", "shard")),
        P(("grp", "shard"), None),
        P(("grp", "shard"), None, None),
        P(("grp", "shard"), None),
        P(),
        P(),
        P(),
        P(),
        P(),
        P(("grp", "shard"), None),
    )
    return jax.shard_map(
        shards,
        mesh=mesh,
        in_specs=placed,
        out_specs=(
            P("grp", "shard", None),
            P("grp", None),
            P("grp"),
            P("grp", None),
            P("grp"),
            P("grp"),
        ),
        check_vma=False,
    )
```

```python
import jax
import jax.numpy as jnp
from jax import lax
from jax.experimental import pallas as pl
from jax.experimental.pallas import tpu as pltpu
from jax.sharding import PartitionSpec as P

ROWS_DEV = 2048
E = 128
OWNERS = 48
HALF = 24
BLOCK = 32
NX = 4
PIECE = 6
SLOTS = 1024
VMEM_LIMIT = 24 * 1024 * 1024


def in_hbm(*values):
    return [pltpu.with_memory_space_constraint(v, pltpu.HBM) for v in values]


def iota(shape, dim):
    return lax.broadcasted_iota(jnp.int32, shape, dim)


def split(rows):
    high = rows.astype(jnp.bfloat16)
    low = (rows - high.astype(jnp.float32)).astype(jnp.bfloat16)
    return jnp.concatenate([high, low], axis=1)


CHUNK = 512
QUARTER = 24
SIDE = 2 * QUARTER
PART = NX * QUARTER


def sigmoid(z):
    return 0.5 * jnp.tanh(0.5 * z) + 0.5


def place(g, side):
    core, y0, y1, y2 = g & 1, (g >> 1) & 1, (g >> 2) & 1, (g >> 3) & 1
    return side * 16 + core * 8 + y0 * 4 + (y1 ^ y2) * 2 + y2


def dense_kernel(
    target_ref, lengths_in, hist_in, pg_in, w1_in, b1_in, w2_in, b2_in, w3_in, ids_in, blocks_in,
    drow_ref, part_ref, ids_ref, blocks_ref,
    lengths_ref, hist_ref, pg_ref, w1_ref, b1_ref, w2_ref, b2_ref, w3_ref,
    feats, act1s, dz2s, dz1s, sems,
):
    inputs = (hist_in, w1_in, b1_in, w2_in, b2_in, w3_in, pg_in, lengths_in, ids_in, blocks_in)
    held = (hist_ref, w1_ref, b1_ref, w2_ref, b2_ref, w3_ref, pg_ref, lengths_ref, ids_ref, blocks_ref)
    copies = [pltpu.make_async_copy(a, b, sems.at[k]) for k, (a, b) in enumerate(zip(inputs, held))]
    for copy in copies:
        copy.start()
    for copy in copies:
        copy.wait()
    query = target_ref[...]
    w1, w2, w3 = w1_ref[...], w2_ref[...], w3_ref[...]
    grad_w3 = jnp.zeros((1, E), jnp.float32)
    grad_b2 = jnp.zeros((1, E), jnp.float32)
    grad_b1 = jnp.zeros((1, 2 * E), jnp.float32)
    samples = CHUNK // 128
    across = (((1,), (1,)), ((), ()))
    down = (((0,), (0,)), ((), ()))
    for c in range(SLOTS // CHUNK):
        rows = slice(c * CHUNK, (c + 1) * CHUNK)
        hist_low = hist_ref[rows, :]
        hist = hist_low.astype(jnp.float32)
        def spread(rows_of):
            parts = [rows_of[b : b + 1, :] for b in range(c * samples, (c + 1) * samples)]
            return jnp.concatenate([jnp.broadcast_to(v, (128, E)) for v in parts], axis=0)
        q = spread(query)
        pg = spread(pg_ref)
        live = jnp.concatenate(
            [iota((128, 1), 0) < lengths_ref[b] for b in range(c * samples, (c + 1) * samples)], axis=0
        )
        feat = jnp.concatenate(
            [q.astype(jnp.bfloat16), hist_low, (q - hist).astype(jnp.bfloat16), (q * hist).astype(jnp.bfloat16)],
            axis=1,
        )
        feats[rows, :] = feat
        act1 = sigmoid(jnp.dot(feat, w1, preferred_element_type=jnp.float32) + b1_ref[...])
        act1_low = act1.astype(jnp.bfloat16)
        act1s[rows, :] = act1_low
        act2 = sigmoid(jnp.dot(act1_low, w2, preferred_element_type=jnp.float32) + b2_ref[...])
        score = jnp.where(live, jnp.sum(act2 * w3, axis=1, keepdims=True), 0.0)
        dscore = jnp.where(live, jnp.sum(pg * hist, axis=1, keepdims=True), 0.0)
        dact2 = dscore * act2
        grad_w3 += jnp.sum(dact2, axis=0, keepdims=True)
        dz2_full = dact2 * w3 * (1.0 - act2)
        grad_b2 += jnp.sum(dz2_full, axis=0, keepdims=True)
        dz2 = dz2_full.astype(jnp.bfloat16)
        dz2s[rows, :] = dz2
        back = lax.dot_general(dz2, w2, across, preferred_element_type=jnp.float32)
        dz1_full = back * act1 * (1.0 - act1)
        grad_b1 += jnp.sum(dz1_full, axis=0, keepdims=True)
        dz1 = dz1_full.astype(jnp.bfloat16)
        dz1s[rows, :] = dz1
        dfeat = lax.dot_general(dz1, w1[E:, :], across, preferred_element_type=jnp.float32)
        drow_ref[rows, :] = dfeat[:, :E] - dfeat[:, E : 2 * E] + dfeat[:, 2 * E :] * q + score * pg

    grad_w1 = lax.dot_general(feats[...], dz1s[...], down, preferred_element_type=jnp.float32)
    grad_w2 = lax.dot_general(act1s[...], dz2s[...], down, preferred_element_type=jnp.float32)
    sub = iota((8, E), 0)
    small = jnp.where(sub == 0, grad_b1[:, :E], jnp.where(sub == 1, grad_b1[:, E:], 0.0))
    small = jnp.where(sub == 2, grad_b2, jnp.where(sub == 3, grad_w3, small))
    for g in range(16):
        for k in range(NX):
            base = place(g, k // 2) * SIDE + (k % 2) * QUARTER
            top = 32 * g + 16 * (k % 2)
            side = E * (k // 2)
            part_ref[base : base + 16, :] = grad_w1[top : top + 16, side : side + E]
            if k < 2:
                last = grad_w2[16 * g + 8 * k : 16 * g + 8 * k + 8, :]
            else:
                last = small
            part_ref[base + 16 : base + 24, :] = last


def dense(lengths, target, hist, pg, w1, b1, w2, b2, w3, ids, blocks):
    whole = pl.BlockSpec(memory_space=pltpu.VMEM)
    return pl.pallas_call(
        dense_kernel,
        out_shape=[
            jax.ShapeDtypeStruct((SLOTS, E), jnp.float32),
            jax.ShapeDtypeStruct((16 * PART, E), jnp.float32),
            jax.ShapeDtypeStruct(ids.shape, ids.dtype),
            jax.ShapeDtypeStruct(blocks.shape, blocks.dtype),
        ],
        in_specs=[whole] + [pl.BlockSpec(memory_space=pltpu.HBM)] * 10,
        out_specs=[whole] * 4,
        scratch_shapes=[pltpu.SMEM(lengths.shape, lengths.dtype)]
        + [pltpu.VMEM(v.shape, v.dtype) for v in (hist, pg, w1, b1, w2, b2, w3)]
        + [
            pltpu.VMEM((SLOTS, 4 * E), jnp.bfloat16),
            pltpu.VMEM((SLOTS, 2 * E), jnp.bfloat16),
            pltpu.VMEM((SLOTS, E), jnp.bfloat16),
            pltpu.VMEM((SLOTS, 2 * E), jnp.bfloat16),
            pltpu.SemaphoreType.DMA((10,)),
        ],
        compiler_params=pltpu.CompilerParams(vmem_limit_bytes=VMEM_LIMIT),
        cost_estimate=pl.CostEstimate(
            flops=1_100_000_000, bytes_accessed=2_200_000, transcendentals=400_000
        ),
        name="dense",
    )(target, *in_hbm(lengths, hist, pg, w1, b1, w2, b2, w3, ids, blocks))


def pack_kernel(
    me_ref, counts_in, drow_ref, ids_ref, blocks_ref, send_ref, counts_ref, pick, source, sem
):
    fetch = pltpu.make_async_copy(counts_in, counts_ref, sem)
    fetch.start()
    me = me_ref[0]

    source[:, : 2 * E] = split(drow_ref[...])
    ids = ids_ref[...] & (ROWS_DEV - 1)
    id_columns = jnp.transpose(ids.astype(jnp.float32))
    for b in range(8):
        column = jnp.broadcast_to(id_columns[:, b : b + 1], (128, 128)).astype(jnp.int32)
        source[b * 128 : (b + 1) * 128, 2 * E : 3 * E] = (column >> 8).astype(jnp.float32).astype(jnp.bfloat16)
        source[b * 128 : (b + 1) * 128, 3 * E :] = (column & 255).astype(jnp.float32).astype(jnp.bfloat16)

    slot = iota((8, SLOTS), 1).astype(jnp.float32)[:1]
    eye = iota((HALF, OWNERS), 0) == iota((HALF, OWNERS), 1)
    def one_hot(mask, row):
        chosen = jnp.where(mask, row.astype(jnp.float32), 0.0)
        column = jnp.sum(chosen, axis=1, keepdims=True)
        return jnp.where(column == slot, 1.0, 0.0)
    for o in range(0, OWNERS, 2):
        pair = [one_hot(eye, blocks_ref[k : k + 1, :]) for k in (o, o + 1)]
        pick[o * HALF : (o + 2) * HALF, :] = jnp.concatenate(pair, axis=0).astype(jnp.bfloat16)
    fetch.wait()
    hot = jnp.int32(0)
    for o in range(OWNERS):
        hot = jnp.where(counts_ref[0, o] > HALF, jnp.int32(o), hot)
    r, lane = iota((32, OWNERS), 0), iota((32, OWNERS), 1)
    late = (lane == HALF + PIECE * (r // 8) + r % 8) & (r % 8 < PIECE)
    last = one_hot(late, blocks_ref[pl.ds(hot, 1), :])
    pick[OWNERS * HALF :, :] = last.astype(jnp.bfloat16)

    got = jnp.dot(pick[...], source[...], preferred_element_type=jnp.float32)

    sub, lane = iota((HALF, E), 0), iota((HALF, E), 1)
    place = lane - sub == (me % NX) * BLOCK
    sub8, lane8 = iota((8, E), 0), iota((8, E), 1)
    place8 = (lane8 - sub8 == (me % 16) * 8) & (sub8 < PIECE)
    tails = []
    for x in range(NX):
        part = got[OWNERS * HALF + 8 * x : OWNERS * HALF + 8 * x + 8]
        where_to = part[:, 2 * E : 3 * E] * 256.0 + part[:, 3 * E :] + 1.0
        row = jnp.sum(jnp.where(place8, where_to, 0.0), axis=0, keepdims=True)
        tails.append(jnp.where(sub8 < PIECE, part[:, :E] + part[:, E : 2 * E], row))
    for o in range(OWNERS):
        part = got[o * HALF : (o + 1) * HALF]
        send_ref[o, :HALF, :] = part[:, :E] + part[:, E : 2 * E]
        where_to = part[:, 2 * E : 3 * E] * 256.0 + part[:, 3 * E :] + 1.0
        used = place & (sub < counts_ref[0, o])
        row = jnp.sum(jnp.where(used, where_to, 0.0), axis=0, keepdims=True)
        send_ref[o, HALF:, :] = jnp.where(sub8 == PIECE, row, tails[o % NX])


def pack(me, counts, drow, ids, blocks):
    whole = pl.BlockSpec(memory_space=pltpu.VMEM)
    scalar = pl.BlockSpec(memory_space=pltpu.SMEM)
    return pl.pallas_call(
        pack_kernel,
        out_shape=jax.ShapeDtypeStruct((OWNERS, BLOCK, E), jnp.float32),
        in_specs=[scalar, pl.BlockSpec(memory_space=pltpu.HBM), whole, whole, whole],
        out_specs=whole,
        scratch_shapes=[
            pltpu.SMEM(counts.shape, counts.dtype),
            pltpu.VMEM((OWNERS * HALF + 32, SLOTS), jnp.bfloat16),
            pltpu.VMEM((SLOTS, 4 * E), jnp.bfloat16),
            pltpu.SemaphoreType.DMA(()),
        ],
        compiler_params=pltpu.CompilerParams(vmem_limit_bytes=VMEM_LIMIT),
        cost_estimate=pl.CostEstimate(
            flops=2 * 1184 * 1024 * 512, bytes_accessed=2_000_000, transcendentals=0
        ),
        name="pack",
    )(me, *in_hbm(counts), drow, ids, blocks)


STEP = 512


def product(t, dest, rows):
    table_row = (iota((STEP, E), 0) + (t * STEP + 1)).astype(jnp.float32)
    hits = [
        jnp.where(table_row == dest[0:1, k : k + 128], 1.0, 0.0).astype(jnp.bfloat16)
        for k in range(0, OWNERS * BLOCK, 128)
    ]
    both = jnp.dot(jnp.concatenate(hits, axis=1), rows[...], preferred_element_type=jnp.float32)
    return both[:, :E] + both[:, E:]


SCATTER_SCRATCH = [
    pltpu.VMEM((OWNERS * BLOCK, 2 * E), jnp.bfloat16),
    pltpu.VMEM((8, OWNERS * BLOCK), jnp.float32),
]
SCATTER_COST = pl.CostEstimate(flops=2 * 2048 * 1536 * 256, bytes_accessed=2_500_000, transcendentals=0)


def add_main_kernel(got_ref, table_ref, rows, dest):
    for g in range(OWNERS // NX):
        rows[g * 128 : (g + 1) * 128, :] = split(got_ref[g * 128 : (g + 1) * 128, :])
        total = sum(got_ref[(NX * g + j) * BLOCK + HALF : (NX * g + j + 1) * BLOCK, :] for j in range(NX))
        dest[:, g * 128 : (g + 1) * 128] = jnp.broadcast_to(total[PIECE : PIECE + 1, :], (8, E))
    for t in range(ROWS_DEV // STEP):
        table_ref[t * STEP : (t + 1) * STEP, :] = product(t, dest, rows)


def add_main(got):
    whole = pl.BlockSpec(memory_space=pltpu.VMEM)
    return pl.pallas_call(
        add_main_kernel,
        out_shape=jax.ShapeDtypeStruct((ROWS_DEV, E), jnp.float32),
        in_specs=[whole],
        out_specs=whole,
        scratch_shapes=SCATTER_SCRATCH,
        compiler_params=pltpu.CompilerParams(vmem_limit_bytes=VMEM_LIMIT),
        cost_estimate=SCATTER_COST,
        name="add_main",
    )(got)


def add_late_kernel(
    me_ref, counts_ref, table_in, own_in, late0_in, late1_in, late2_in, table_out,
    table, late, rows, dest, sems,
):
    @pl.when(counts_ref[0, me_ref[0]] > HALF)
    def _():
        slabs = (own_in, late0_in, late1_in, late2_in)
        fetches = [pltpu.make_async_copy(slabs[k], late.at[k], sems.at[k]) for k in range(NX)]
        fetches.append(pltpu.make_async_copy(table_in, table, sems.at[NX]))
        for fetch in fetches:
            fetch.start()
        for fetch in fetches:
            fetch.wait()
        for k in range(NX):
            for g in range(3):
                tiles = [late[k, s * 8 : s * 8 + 8, :] for s in range(16 * g, 16 * g + 16)]
                at = (k * 3 + g) * 128
                rows[at : at + 128, :] = split(jnp.concatenate(tiles, axis=0))
                dest[:, at : at + 128] = jnp.broadcast_to(sum(tiles)[7:8, :], (8, E))
        for t in range(ROWS_DEV // STEP):
            table[t * STEP : (t + 1) * STEP, :] += product(t, dest, rows)
        write = pltpu.make_async_copy(table, table_out, sems.at[NX])
        write.start()
        write.wait()


def add_late(me, counts, table, late):
    scalar = pl.BlockSpec(memory_space=pltpu.SMEM)
    anywhere = pl.BlockSpec(memory_space=pl.ANY)
    return pl.pallas_call(
        add_late_kernel,
        out_shape=jax.ShapeDtypeStruct((ROWS_DEV, E), jnp.float32),
        in_specs=[scalar, scalar] + [anywhere] * 5,
        out_specs=anywhere,
        scratch_shapes=[
            pltpu.VMEM((ROWS_DEV, E), jnp.float32),
            pltpu.VMEM((NX, OWNERS * 8, E), jnp.float32),
        ]
        + SCATTER_SCRATCH
        + [pltpu.SemaphoreType.DMA((NX + 1,))],
        input_output_aliases={2: 0},
        compiler_params=pltpu.CompilerParams(vmem_limit_bytes=VMEM_LIMIT),
        cost_estimate=SCATTER_COST,
        name="add_late",
    )(me, counts, table, *late)


STEPS = (("shard", 1), ("grp", 1), ("grp", 2), ("grp", 4), ("grp", 12))
NZ = OWNERS // NX
Z_GROUPS = [[z * NX + x for z in range(NZ)] for x in range(NX)]


def swap(value, axis, bits):
    size = lax.axis_size(axis)
    return lax.ppermute(value, axis, [(i, i ^ bits) for i in range(size)])


def join_kernel(keep_ref, there_ref, got_ref, copies_ref, slab_ref):
    part = keep_ref[...] + there_ref[...]
    for z in range(NZ):
        copies_ref[z] = part
    for s in range(OWNERS):
        slab_ref[s * 8 : s * 8 + 8, :] = got_ref[s * BLOCK + HALF : (s + 1) * BLOCK, :]


def join(keep, there, got):
    whole = pl.BlockSpec(memory_space=pltpu.VMEM)
    return pl.pallas_call(
        join_kernel,
        out_shape=[
            jax.ShapeDtypeStruct((NZ, SIDE, E), jnp.float32),
            jax.ShapeDtypeStruct((OWNERS * 8, E), jnp.float32),
        ],
        in_specs=[whole, whole, whole],
        out_specs=[whole, whole],
        compiler_params=pltpu.CompilerParams(vmem_limit_bytes=VMEM_LIMIT),
        cost_estimate=pl.CostEstimate(flops=3072, bytes_accessed=1_300_000, transcendentals=0),
        name="join",
    )(keep, there, got)


def add_kernel_z(parts_ref, out_ref):
    part = parts_ref[0]
    for z in range(1, NZ):
        part += parts_ref[z]
    out_ref[...] = part


def add_parts(parts):
    whole = pl.BlockSpec(memory_space=pltpu.VMEM)
    return pl.pallas_call(
        add_kernel_z,
        out_shape=jax.ShapeDtypeStruct((SIDE, E), jnp.float32),
        in_specs=[whole],
        out_specs=whole,
        compiler_params=pltpu.CompilerParams(vmem_limit_bytes=VMEM_LIMIT),
        cost_estimate=pl.CostEstimate(flops=67584, bytes_accessed=320_000, transcendentals=0),
        name="add_parts",
    )(parts)


def final_kernel(g_ref, side_ref, mine_ref, other_ref, w1_ref, b1_ref, w2_ref, b2_ref, w3_ref):
    g, first = g_ref[0], side_ref[0] == 0
    mine, other = mine_ref[...], other_ref[...]
    low, high = jnp.where(first, mine, other), jnp.where(first, other, mine)
    quarters = [low[:QUARTER], low[QUARTER:], high[:QUARTER], high[QUARTER:]]
    for k in range(NX):
        top, side = 16 * (k % 2), E * (k // 2)
        w1_ref[top : top + 16, side : side + E] = quarters[k][:16]
    w2_ref[:8, :] = quarters[0][16:]
    w2_ref[8:, :] = quarters[1][16:]
    small = quarters[2][16:]
    by16 = pltpu.roll(small, (128 - (g % 8) * 16) % 128, 1)
    by8 = pltpu.roll(small, (128 - g * 8) % 128, 1)
    b1_ref[...] = jnp.where(g < 8, by16[0:1, :16], by16[1:2, :16])
    b2_ref[...] = by8[2:3, :8]
    w3_ref[...] = by8[3:4, :8]


def final(g, side, mine, other):
    whole = pl.BlockSpec(memory_space=pltpu.VMEM)
    shapes = ((32, 2 * E), (1, 16), (16, E), (1, 8), (1, 8))
    return pl.pallas_call(
        final_kernel,
        out_shape=[jax.ShapeDtypeStruct(shape, jnp.float32) for shape in shapes],
        in_specs=[pl.BlockSpec(memory_space=pltpu.SMEM)] * 2 + [whole, whole],
        out_specs=[whole] * 5,
        compiler_params=pltpu.CompilerParams(vmem_limit_bytes=VMEM_LIMIT),
        cost_estimate=pl.CostEstimate(flops=1024, bytes_accessed=100_000, transcendentals=0),
        name="final",
    )(g, side, mine, other)


def shards(
    target,
    history,
    lengths,
    hist_ids,
    block_rows,
    block_counts,
    attn_w1,
    attn_b1,
    attn_w2,
    attn_b2,
    attn_w3,
    pooled_gradient,
):
    g = lax.axis_index("grp")
    me = lax.axis_index("shard").reshape(1)
    drow, part, ids, blocks = dense(
        lengths,
        target.astype(jnp.float32),
        history.reshape(SLOTS, E),
        pooled_gradient,
        attn_w1,
        attn_b1.reshape(1, 2 * E),
        attn_w2,
        attn_b2.reshape(1, E),
        attn_w3.reshape(1, E),
        hist_ids,
        block_rows[0],
    )
    send = pack(me, block_counts, drow, ids, blocks)
    got = lax.all_to_all(send, "shard", split_axis=0, concat_axis=0, tiled=True)
    got = got.reshape(OWNERS * BLOCK, E)

    part = part.reshape(2, 2, 2, 2, 2, SIDE, E)
    y2 = (g >> 3) & 1
    side = (me[0] ^ (me[0] >> 1)) & 1
    bits = (side, g & 1, (g >> 1) & 1, ((g >> 2) & 1) ^ y2, y2)
    for bit, (axis, k) in zip(bits, STEPS):
        keep = lax.dynamic_index_in_dim(part, bit, 0, False)
        away = lax.dynamic_index_in_dim(part, 1 - bit, 0, False)
        part = keep + swap(away, axis, k)
    copies, slab = join(part, swap(part, "shard", 3), got)
    parts = lax.all_to_all(
        copies, "shard", split_axis=0, concat_axis=0, tiled=True, axis_index_groups=Z_GROUPS
    )
    total = add_parts(parts)
    other = swap(total, "shard", 1)
    late = [slab]
    for turn in (1, 2, 3):
        pairs = [(s, s // NX * NX + (s + turn) % NX) for s in range(OWNERS)]
        late.append(lax.ppermute(slab, "shard", pairs))
    table = add_late(me, block_counts, add_main(got), late)
    grad_w1, grad_b1, grad_w2, grad_b2, grad_w3 = final(g.reshape(1), side.reshape(1), total, other)
    return (
        table[None],
        grad_w1,
        grad_b1.reshape(16),
        grad_w2,
        grad_b2.reshape(8),
        grad_w3.reshape(8),
    )


def solution(mesh):
    placed = (
        P(("grp", "shard"), None),
        P(("grp", "shard"), None, None),
        P(("grp", "shard")),
        P(("grp", "shard"), None),
        P(("grp", "shard"), None, None),
        P(("grp", "shard"), None),
        P(),
        P(),
        P(),
        P(),
        P(),
        P(("grp", "shard"), None),
    )
    return jax.shard_map(
        shards,
        mesh=mesh,
        in_specs=placed,
        out_specs=(
            P("grp", "shard", None),
            P("grp", None),
            P("grp"),
            P("grp", None),
            P("grp"),
            P("grp"),
        ),
        check_vma=False,
    )
```
